1024 devices in a mesh: wide: 64 (over z, core), rep: 16 (over x, y).
Axes of the slice: x: 4, y: 4, z: 32, core: 2. Of those that a mesh axis runs over, the one named last changes fastest.
Arguments:
- amplitudes: bfloat16 [64, 80, 128, 128], P(None, 'rep', 'wide'), may hold values from -6 to 6
- integrals: bfloat16 [80, 128, 80, 128], P('rep'), may hold values from -0.109375 to 0.109375
- occ_irrep: int32 [80], replicated, may hold values from 0 to 7
- vir_count: int32 [8], replicated, may hold values from 1 to 128, 600 in all
Outputs:
- cycle_block: bfloat16 [64, 128, 80, 128], P('wide', None, 'rep')
The draws below stay inside these ranges and needn't reach their ends.
Inputs may be any that keep to these rules, and one draw needn't show every extreme that they name: `vir_count`: the 8 counts sum to 600; the largest is exactly 128.
All inputs are finite; a program needn't handle non-finite values.
Results may differ from the reference program's by a relative error of at most 0.017.
Values may be sent and summed in bfloat16 or wider, within the bound.
A program may use at most 64 MiB of HBM per device.

```python
import math
import jax
import jax.numpy as jnp
import numpy as np
from jax import lax

O = 80
V = 600
IRREPS = 8
VM = 128
SYM = 3
ROW_OCC = 64
COL_OCC = 80
N_REP = 16


def with_ends(entries, key, least, top_value):
    shape = entries.shape
    spot = [jax.random.randint(jax.random.fold_in(key, axis), (), 0, shape[axis]) for axis in range(len(shape))]
    entries = entries.at[tuple(spot)].set(least)
    longest = shape.index(max(shape))
    spot[longest] = (spot[longest] + 1) % shape[longest]
    return entries.at[tuple(spot)].set(top_value)


def spiked(values, stream_key, source, target, shards_of, factor):
    def block_of(position):
        return (jnp.arange(values.shape[position]) // (values.shape[position] // shards_of)).reshape((-1,) + (1,) * (values.ndim - 1 - position))

    first = jax.random.permutation(stream_key, shards_of)[block_of(target)]
    other_side = (block_of(target) + shards_of // 2) % shards_of
    return jnp.where((block_of(source) == first) | (block_of(source) == other_side), factor * values, values)


def levels(rng, dims, split, least, high):
    level = 1.0
    for position, shards_of in split:
        draws = jax.random.uniform(jax.random.fold_in(jax.random.fold_in(rng, 6), position), (shards_of,), jnp.float32, least / len(split), high / len(split))
        level = level * jnp.repeat(jnp.exp(draws), dims[position] // shards_of).reshape((-1,) + (1,) * (len(dims) - 1 - position))
    return level


def profile(number_of, total, most, slope):
    weights = [(1 << 20) // math.isqrt(standing ** slope) + 1 for standing in range(2, number_of + 1)]
    rest, given = total - most - (number_of - 1), [1] * (number_of - 1)
    while rest > 0:
        candidates = [i for i in range(number_of - 1) if given[i] < most]
        mass, left = sum([weights[i] for i in candidates]), rest
        for i in candidates:
            addition = min(most - given[i], max(1, left * weights[i] // mass), rest)
            given[i] = given[i] + addition
            rest = rest - addition
    return np.array([most] + given)


def uneven(rng, count, total, bound, skew):
    if count == 2:
        one = jax.random.randint(rng, (), max(1, total - bound), min(bound, total - 1) + 1)
        return jnp.stack([one, total - one])
    sizes = jnp.asarray(profile(count, total, bound, skew), jnp.int32)
    twos = (count - 1) // 2
    source_of, taker = sizes[1:1 + 2 * twos:2], sizes[2:2 + 2 * twos:2]
    margin = jnp.minimum(source_of - 1, bound - taker)
    shifted = jax.random.randint(jax.random.fold_in(rng, 1), (twos,), 0, 1 << 20) % (margin + 1)
    sizes = sizes.at[1:1 + 2 * twos:2].set(source_of - shifted).at[2:2 + 2 * twos:2].set(taker + shifted)
    return sizes[jax.random.permutation(jax.random.fold_in(rng, 2), count)]


def noise(own_key, extent, width, reach, cuts=(), kind=jnp.bfloat16):
    array = width * jax.random.normal(own_key, extent, jnp.float32)
    if cuts:
        array = array * levels(own_key, extent, cuts, -0.22, 0.18)
    return jnp.clip(array, -reach, reach).astype(kind)


def noise_with(stream_key, extent, spread, reach, shards, heavy, kind=jnp.bfloat16):
    values = spread * jax.random.normal(stream_key, extent, jnp.float32)
    if shards:
        values = values * levels(stream_key, extent, shards, -0.22, 0.18)
    return jnp.clip(spiked(values, jax.random.fold_in(stream_key, 3), *heavy), -reach, reach).astype(kind)


def setup_inputs(seed: int = 0) -> dict:
    key_of = jax.random.split(jax.random.key(seed), 5)
    return {
        "amplitudes": noise(key_of[0], (ROW_OCC, O, VM, VM), 1.0, 6.0, ((1, 16), (2, 64))),
        "integrals": noise_with(key_of[1], (O, VM, COL_OCC, VM), (O * V // IRREPS) ** -0.5, 0.109375, ((0, 16),), (0, 2, 16, 2.0)),
        "occ_irrep": with_ends(jax.random.randint(key_of[2], (O,), 0, IRREPS), jax.random.fold_in(key_of[2], 1), 0, IRREPS - 1).astype(jnp.int32),
        "vir_count": uneven(key_of[3], IRREPS, V, VM, 1).astype(jnp.int32),
    }


def counts_for(occ_irrep, vir_count):
    target = jnp.bitwise_xor(occ_irrep, SYM)
    irreps = jnp.arange(IRREPS, dtype=jnp.int32)
    picked = jnp.where(target[:, None] == irreps[None, :], vir_count[None, :], 0)
    return jnp.sum(picked, axis=1)


def reference(amplitudes, integrals, occ_irrep, vir_count):
    per_occ = counts_for(occ_irrep, vir_count)
    vir_slots = jnp.arange(VM, dtype=jnp.int32)
    valid = per_occ[:, None] > vir_slots[None, :]
    masked = jnp.where(valid[None, :, None, :], amplitudes, jnp.zeros((), amplitudes.dtype))
    occ_block = O // N_REP
    summed = jnp.zeros((ROW_OCC, VM, COL_OCC, VM), jnp.float32)
    for block in range(N_REP):
        piece = masked[:, block * occ_block:(block + 1) * occ_block].astype(jnp.float32)
        weights = integrals[block * occ_block:(block + 1) * occ_block].astype(jnp.float32)
        partial_value = jnp.einsum("ikac,kcjb->iajb", piece, weights)
        rounded = lax.optimization_barrier(partial_value.astype(jnp.bfloat16))
        summed = summed + rounded.astype(jnp.float32)
    row_valid = valid[:ROW_OCC].astype(jnp.float32)
    col_valid = valid[:COL_OCC].astype(jnp.float32)
    result = summed * row_valid[:, :, None, None] * col_valid[None, None, :, :]
    return result.astype(jnp.bfloat16)
```

```python
import jax
import jax.numpy as jnp
from jax import lax
from jax.experimental import pallas as pl
from jax.experimental.pallas import tpu as pltpu
from jax.sharding import PartitionSpec as P

SYM = 3
MESH = pl.DeviceIdType.MESH
F32 = jnp.float32
BF16 = jnp.bfloat16

WIDE = 64
GROUP = 8
SLOTS = 128
SIDE = 4
K_LOCAL = 5
J_LOCAL = 5
CHUNKS = ((-1, 0, 1, 2), (3, 4, 5, 6))


def to_f32(value):
    return value.astype(F32)


def kernel(
    amps_hbm, ints_hbm, occ_ref, vir_ref, out_ref,
    amps, slots_in, raw, weights, rows, part, first_in, second_in, mid, third_in, fourth_in,
    load_sems, own_sem, spread_send, spread_recv, main_send, first_recv, second_recv,
    side_send, third_recv, fourth_recv,
):
    wide = lax.axis_index("wide")
    rep = lax.axis_index("rep")
    x, y = rep // SIDE, rep % SIDE
    group = wide // GROUP

    amps_load = pltpu.make_async_copy(amps_hbm, amps, load_sems.at[K_LOCAL])
    amps_load.start()
    int_loads = [
        pltpu.make_async_copy(ints_hbm.at[k], raw.at[k], load_sems.at[k])
        for k in range(K_LOCAL)
    ]
    for load in int_loads:
        load.start()

    def along(axis, step):
        if axis == 0:
            other = lax.rem(x + step + SIDE, SIDE) * SIDE + y
        else:
            other = x * SIDE + lax.rem(y + step + SIDE, SIDE)
        return {"wide": wide, "rep": other}

    barrier = pltpu.get_barrier_semaphore()

    def greet(step, carry):
        peer = lax.rem(wide + step, WIDE)
        pl.semaphore_signal(
            barrier, inc=1, device_id={"wide": peer, "rep": rep}, device_id_type=MESH
        )
        return carry

    for axis in range(2):
        for step in (1, -1):
            pl.semaphore_signal(
                barrier, inc=1, device_id=along(axis, step), device_id_type=MESH
            )
    lax.fori_loop(1, WIDE, greet, 0)
    amps_load.wait()
    own = pltpu.make_async_copy(amps.at[wide], slots_in.at[wide], own_sem)
    own.start()
    pl.semaphore_wait(barrier, WIDE - 1 + 4)

    def spread(chunk, first, last, peer_of):
        def send(step, carry):
            peer = peer_of(step)
            pltpu.make_async_remote_copy(
                src_ref=amps.at[peer],
                dst_ref=slots_in.at[wide],
                send_sem=spread_send,
                recv_sem=spread_recv.at[chunk],
                device_id={"wide": peer, "rep": rep},
                device_id_type=MESH,
            ).start()
            return carry

        lax.fori_loop(first, last, send, 0)

    for chunk, sources in enumerate(CHUNKS):
        for source in sorted(sources, key=lambda s: min(s % 8, -s % 8)):
            base = lax.rem(group + (GROUP - source) + GROUP, GROUP) * GROUP
            if source == 0:
                inside = wide - group * GROUP
                spread(chunk, 1, GROUP, lambda s: base + lax.rem(inside + s, GROUP))
            else:
                spread(chunk, 0, GROUP, lambda s, base=base: base + s)

    for k in range(K_LOCAL):
        int_loads[k].wait()

        def turn(step, carry, k=k):
            c = pl.multiple_of(step * 16, 16)
            to = pl.multiple_of(k * SLOTS + step * 16, 16)
            for q in range(5):
                block = raw[k, pl.ds(c, 16), 16 * q : 16 * q + 16, :]
                weights[16 * q : 16 * q + 16, pl.ds(to, 16), :] = jnp.swapaxes(block, 0, 1)
            return carry

        lax.fori_loop(0, SLOTS // 16, turn, 0)

    lane = lax.broadcasted_iota(jnp.int32, (16, SLOTS), 1)
    row = lax.broadcasted_iota(jnp.int32, (16, SLOTS), 0)

    def count_of(orbital):
        return vir_ref[jnp.bitwise_xor(occ_ref[orbital], SYM)]

    def absolute(chunk, place):
        return lax.rem(group + CHUNKS[chunk][place] + GROUP, GROUP)

    def wait_slots(chunk):
        many = 31 if chunk == 0 else 32
        pltpu.make_async_remote_copy(
            src_ref=amps.at[pl.ds(0, many)],
            dst_ref=slots_in.at[pl.ds(0, many)],
            send_sem=spread_send,
            recv_sem=spread_recv.at[chunk],
            device_id=along(0, 1),
            device_id_type=MESH,
        ).wait_recv()
        if chunk == 0:
            own.wait()

    def gather_rows(chunk):
        for k in range(K_LOCAL):
            valid = lane < count_of(rep * K_LOCAL + k)
            for place in range(4):
                at = pl.multiple_of(absolute(chunk, place) * GROUP, GROUP)
                block = slots_in[pl.ds(at, GROUP), k, :, :].reshape(16, SLOTS)
                rows[chunk, 16 * place : 16 * place + 16, SLOTS * k : SLOTS * k + SLOTS] = (
                    jnp.where(valid, to_f32(block), 0.0).astype(BF16)
                )

    sent = []

    def send(src, dst, sems, index, recv, device):
        copy = pltpu.make_async_remote_copy(
            src_ref=src,
            dst_ref=dst,
            send_sem=sems.at[index],
            recv_sem=recv,
            device_id=device,
            device_id_type=MESH,
        )
        copy.start()
        sent.append(copy)
        return copy

    def multiply(chunk):
        for dx in (2, 1, 3, 0):

            def pair(t, carry, dx=dx):
                pieces = []
                ways = (2 + t, 1 - t)
                for dy in ways:
                    target = lax.rem(x + dx, SIDE) * SIDE + lax.rem(y + dy, SIDE)
                    pieces += [weights[target * J_LOCAL + j] for j in range(J_LOCAL)]
                product = jnp.dot(
                    rows[chunk], jnp.concatenate(pieces, axis=1), preferred_element_type=F32
                ).astype(BF16)
                for n, dy in enumerate(ways):
                    for j in range(J_LOCAL):
                        at = (n * J_LOCAL + j) * SLOTS
                        part[chunk, 0, dx, dy, j] = product[:32, at : at + SLOTS]
                        part[chunk, 1, dy, dx, j] = product[32:, at : at + SLOTS]
                return carry

            lax.fori_loop(0, 2, pair, 0)
            base = chunk * 16
            if dx == 2:
                for d, half in ((0, 0), (1, 2)):
                    send(
                        part.at[chunk, 0, 2, pl.ds(half, 2)], first_in.at[chunk, 0, d],
                        main_send, base + d, first_recv.at[chunk, 0, d], along(0, 1 - 2 * d),
                    )
            if dx in (1, 3):
                d, half = (0, 2) if dx == 1 else (1, 0)
                send(
                    part.at[chunk, 0, dx, pl.ds(half, 2)],
                    second_in.at[chunk, 0, d, pl.ds(half, 2)],
                    main_send, base + 2 + d, second_recv.at[chunk, 0, d, 0], along(0, 1 - 2 * d),
                )
            d = 0 if dx < 2 else 1
            send(
                part.at[chunk, 1, 2, dx], first_in.at[chunk, 1, d, dx % 2],
                main_send, base + 4 + dx, first_recv.at[chunk, 1, d], along(1, 1 - 2 * d),
            )
            send(
                part.at[chunk, 1, 1 if d else 3, dx], second_in.at[chunk, 1, 1 - d, dx],
                main_send, base + 8 + dx, second_recv.at[chunk, 1, 1 - d, 0], along(1, 2 * d - 1),
            )

    def wait_for(buffer, sem):
        pltpu.make_async_remote_copy(
            src_ref=buffer, dst_ref=buffer, send_sem=own_sem, recv_sem=sem,
            device_id=along(0, 1), device_id_type=MESH,
        ).wait_recv()

    def pass_on(chunk):
        for way in range(2):
            for d in range(2):
                dp, half = (1, 0) if d == 0 else (3, 2)
                wait_for(first_in.at[chunk, way, d], first_recv.at[chunk, way, d])
                part[chunk, way, dp, half : half + 2] = (
                    to_f32(part[chunk, way, dp, half : half + 2]) + to_f32(first_in[chunk, way, d])
                ).astype(BF16)
                send(
                    part.at[chunk, way, dp, pl.ds(half, 2)],
                    second_in.at[chunk, way, d, pl.ds(half, 2)],
                    main_send, chunk * 16 + 12 + 2 * way + d,
                    second_recv.at[chunk, way, d, 1], along(way, 1 - 2 * d),
                )

    def turn_corner(chunk):
        for way in range(2):
            for d in range(2):
                for late in range(2):
                    half = 2 * ((1 - late + d) % 2)
                    wait_for(
                        second_in.at[chunk, way, d, pl.ds(half, 2)],
                        second_recv.at[chunk, way, d, late],
                    )
            for ds in (2, 1, 3, 0):
                total = (
                    to_f32(part[chunk, way, 0, ds])
                    + to_f32(second_in[chunk, way, 0, ds])
                    + to_f32(second_in[chunk, way, 1, ds])
                ).astype(BF16)
                mid[chunk, way, ds, 0] = total[:, :16]
                mid[chunk, way, ds, 1] = total[:, 16:]
                base = chunk * 12 + way * 6
                axis = 1 - way
                if ds == 2:
                    for d in range(2):
                        send(
                            mid.at[chunk, way, 2, d], third_in.at[chunk, way, d],
                            side_send, base + d, third_recv.at[chunk, way, d],
                            along(axis, 1 - 2 * d),
                        )
                if ds in (1, 3):
                    d, h = (0, 1) if ds == 1 else (1, 0)
                    send(
                        mid.at[chunk, way, ds, h], fourth_in.at[chunk, way, d, h],
                        side_send, base + 2 + d, fourth_recv.at[chunk, way, d, h],
                        along(axis, 1 - 2 * d),
                    )

    def pass_on_side(chunk):
        for way in range(2):
            for d in range(2):
                ds = 1 if d == 0 else 3
                wait_for(third_in.at[chunk, way, d], third_recv.at[chunk, way, d])
                mid[chunk, way, ds, d] = (
                    to_f32(mid[chunk, way, ds, d]) + to_f32(third_in[chunk, way, d])
                ).astype(BF16)
                send(
                    mid.at[chunk, way, ds, d], fourth_in.at[chunk, way, d, d],
                    side_send, chunk * 12 + way * 6 + 4 + d, fourth_recv.at[chunk, way, d, d],
                    along(1 - way, 1 - 2 * d),
                )

    def finish(chunk):
        row_count = count_of(wide)
        for way in range(2):
            for d in range(2):
                for h in range(2):
                    wait_for(fourth_in.at[chunk, way, d, h], fourth_recv.at[chunk, way, d, h])
            for h in range(2):
                at = pl.multiple_of(absolute(chunk, 2 * way + h) * 16, 16)
                for j in range(J_LOCAL):
                    total = (
                        to_f32(mid[chunk, way, 0, h, j])
                        + to_f32(fourth_in[chunk, way, 0, h, j])
                        + to_f32(fourth_in[chunk, way, 1, h, j])
                    )
                    valid = (row + at < row_count) & (lane < count_of(rep * J_LOCAL + j))
                    out_ref[j, pl.ds(at, 16), :] = jnp.where(valid, total, 0.0).astype(BF16)

    wait_slots(0)
    gather_rows(0)
    multiply(0)
    pass_on(0)
    turn_corner(0)
    wait_slots(1)
    gather_rows(1)
    multiply(1)
    pass_on_side(0)
    pass_on(1)
    finish(0)
    turn_corner(1)
    pass_on_side(1)
    finish(1)

    pltpu.make_async_remote_copy(
        src_ref=amps.at[pl.ds(0, WIDE - 1)],
        dst_ref=slots_in.at[pl.ds(0, WIDE - 1)],
        send_sem=spread_send,
        recv_sem=spread_recv.at[0],
        device_id=along(0, 1),
        device_id_type=MESH,
    ).wait_send()
    for copy in sent:
        copy.wait_send()


def body(amplitudes, integrals, occ_irrep, vir_count):
    dma = pltpu.SemaphoreType.DMA
    out = pl.pallas_call(
        kernel,
        out_shape=jax.ShapeDtypeStruct((J_LOCAL, SLOTS, SLOTS), BF16),
        in_specs=[
            pl.BlockSpec(memory_space=pl.ANY),
            pl.BlockSpec(memory_space=pl.ANY),
            pl.BlockSpec(memory_space=pltpu.SMEM),
            pl.BlockSpec(memory_space=pltpu.SMEM),
        ],
        out_specs=pl.BlockSpec(memory_space=pltpu.VMEM),
        scratch_shapes=[
            pltpu.VMEM((WIDE, K_LOCAL, 2, SLOTS), BF16),
            pltpu.VMEM((WIDE, K_LOCAL, 2, SLOTS), BF16),
            pltpu.VMEM((K_LOCAL, SLOTS, 80, SLOTS), BF16),
            pltpu.VMEM((80, K_LOCAL * SLOTS, SLOTS), BF16),
            pltpu.VMEM((2, 64, K_LOCAL * SLOTS), BF16),
            pltpu.VMEM((2, 2, 4, 4, J_LOCAL, 32, SLOTS), BF16),
            pltpu.VMEM((2, 2, 2, 2, J_LOCAL, 32, SLOTS), BF16),
            pltpu.VMEM((2, 2, 2, 4, J_LOCAL, 32, SLOTS), BF16),
            pltpu.VMEM((2, 2, 4, 2, J_LOCAL, 16, SLOTS), BF16),
            pltpu.VMEM((2, 2, 2, J_LOCAL, 16, SLOTS), BF16),
            pltpu.VMEM((2, 2, 2, 2, J_LOCAL, 16, SLOTS), BF16),
            dma((K_LOCAL + 1,)),
            dma,
            dma,
            dma((2,)),
            dma((32,)),
            dma((2, 2, 2)),
            dma((2, 2, 2, 2)),
            dma((24,)),
            dma((2, 2, 2)),
            dma((2, 2, 2, 2)),
        ],
        compiler_params=pltpu.CompilerParams(
            collective_id=0, has_side_effects=True, vmem_limit_bytes=52 * 2**20
        ),
        cost_estimate=pl.CostEstimate(
            flops=2 * 128 * 640 * 10240, bytes_accessed=14 * 2**20, transcendentals=0
        ),
    )(amplitudes, integrals, occ_irrep, vir_count)
    return out.transpose(1, 0, 2)[None]


def solution(mesh):
    in_specs = (P(None, "rep", "wide", None), P("rep", None, None, None), P(), P())
    out_specs = P("wide", None, "rep", None)
    return jax.shard_map(body, mesh=mesh, in_specs=in_specs, out_specs=out_specs, check_vma=False)
```

```python
import jax
import jax.numpy as jnp
from jax import lax
from jax.experimental import pallas as pl
from jax.experimental.pallas import tpu as pltpu
from jax.sharding import PartitionSpec as P

SYM = 3
MESH = pl.DeviceIdType.MESH
F32 = jnp.float32
BF16 = jnp.bfloat16

WIDE = 64
GROUP = 8
SLOTS = 128
SIDE = 4
K_LOCAL = 5
J_LOCAL = 5
CHUNKS = ((4, 3, -3, -2), (2, 1, -1, 0))


def to_f32(value):
    return value.astype(F32)


def kernel(
    amps_hbm, ints_hbm, occ_hbm, vir_hbm, out_ref,
    occ_ref, vir_ref, amps, blocks, blocks_in, raw, weights, rows, part, first_in, second_in, mid, third_in, fourth_in,
    load_sems, own_sem, spread_send, spread_recv, main_send, first_recv, second_recv,
    side_send, third_recv, fourth_recv,
):
    wide = lax.axis_index("wide")
    rep = lax.axis_index("rep")
    x, y = rep // SIDE, rep % SIDE
    group = wide // GROUP

    amps_load = pltpu.make_async_copy(amps_hbm, amps, load_sems.at[K_LOCAL])
    amps_load.start()
    label_loads = [
        pltpu.make_async_copy(occ_hbm, occ_ref, load_sems.at[K_LOCAL + 1]),
        pltpu.make_async_copy(vir_hbm, vir_ref, load_sems.at[K_LOCAL + 2]),
    ]
    for load in label_loads:
        load.start()
    int_loads = [
        pltpu.make_async_copy(ints_hbm.at[k], raw.at[k], load_sems.at[k])
        for k in range(K_LOCAL)
    ]
    for load in int_loads:
        load.start()

    def along(axis, step):
        if axis == 0:
            other = lax.rem(x + step + SIDE, SIDE) * SIDE + y
        else:
            other = x * SIDE + lax.rem(y + step + SIDE, SIDE)
        return {"wide": wide, "rep": other}

    barrier = pltpu.get_barrier_semaphore()

    def greet(step, carry):
        peer = lax.rem(wide + WIDE // 2 + (1 - 2 * (step % 2)) * (step // 2) + WIDE, WIDE)
        pl.semaphore_signal(
            barrier, inc=1, device_id={"wide": peer, "rep": rep}, device_id_type=MESH
        )
        return carry

    for axis in range(2):
        for step in (1, -1):
            pl.semaphore_signal(
                barrier, inc=1, device_id=along(axis, step), device_id_type=MESH
            )
    lax.fori_loop(1, WIDE, greet, 0)
    for k in range(K_LOCAL):
        int_loads[k].wait()

        def turn(step, carry, k=k):
            c = pl.multiple_of(step * 16, 16)
            to = pl.multiple_of(k * SLOTS + step * 16, 16)
            for q in range(5):
                block = raw[k, pl.ds(c, 16), 16 * q : 16 * q + 16, :]
                weights[16 * q : 16 * q + 16, pl.ds(to, 16), :] = jnp.swapaxes(block, 0, 1)
            return carry

        lax.fori_loop(0, SLOTS // 16, turn, 0)

    for load in label_loads:
        load.wait()
    lane = lax.broadcasted_iota(jnp.int32, (16, SLOTS), 1)
    row = lax.broadcasted_iota(jnp.int32, (16, SLOTS), 0)

    def count_of(orbital):
        return vir_ref[jnp.bitwise_xor(occ_ref[orbital], SYM)]

    def target_group(chunk, place):
        return lax.rem(group + CHUNKS[chunk][place] + GROUP, GROUP)

    def gather_rows(chunk):
        for k in range(K_LOCAL):
            valid = lane < count_of(rep * K_LOCAL + k)
            for place in range(4):
                at = pl.multiple_of(target_group(chunk, place) * GROUP, GROUP)
                block = amps[pl.ds(at, GROUP), k, :, :].reshape(16, SLOTS)
                rows[chunk, 16 * place : 16 * place + 16, SLOTS * k : SLOTS * k + SLOTS] = (
                    jnp.where(valid, to_f32(block), 0.0).astype(BF16)
                )

    sent = []

    def send(src, dst, sems, index, recv, device):
        copy = pltpu.make_async_remote_copy(
            src_ref=src,
            dst_ref=dst,
            send_sem=sems.at[index],
            recv_sem=recv,
            device_id=device,
            device_id_type=MESH,
        )
        copy.start()
        sent.append(copy)
        return copy

    def multiply(chunk):
        for dx in (2, 1, 3, 0):

            def pair(t, carry, dx=dx):
                pieces = []
                ways = (2 + t, 1 - t)
                for dy in ways:
                    target = lax.rem(x + dx, SIDE) * SIDE + lax.rem(y + dy, SIDE)
                    pieces += [weights[target * J_LOCAL + j] for j in range(J_LOCAL)]
                product = jnp.dot(
                    rows[chunk], jnp.concatenate(pieces, axis=1), preferred_element_type=F32
                ).astype(BF16)
                for n, dy in enumerate(ways):
                    for j in range(J_LOCAL):
                        at = (n * J_LOCAL + j) * SLOTS
                        part[chunk, 0, dx, dy, j] = product[:32, at : at + SLOTS]
                        part[chunk, 1, dy, dx, j] = product[32:, at : at + SLOTS]
                return carry

            lax.fori_loop(0, 2, pair, 0)
            base = chunk * 16
            if dx == 2:
                for d, half in ((0, 0), (1, 2)):
                    send(
                        part.at[chunk, 0, 2, pl.ds(half, 2)], first_in.at[chunk, 0, d],
                        main_send, base + d, first_recv.at[chunk, 0, d], along(0, 1 - 2 * d),
                    )
            if dx in (1, 3):
                d, half = (0, 2) if dx == 1 else (1, 0)
                send(
                    part.at[chunk, 0, dx, pl.ds(half, 2)],
                    second_in.at[chunk, 0, d, pl.ds(half, 2)],
                    main_send, base + 2 + d, second_recv.at[chunk, 0, d, 0], along(0, 1 - 2 * d),
                )
            d = 0 if dx < 2 else 1
            send(
                part.at[chunk, 1, 2, dx], first_in.at[chunk, 1, d, dx % 2],
                main_send, base + 4 + dx, first_recv.at[chunk, 1, d], along(1, 1 - 2 * d),
            )
            send(
                part.at[chunk, 1, 1 if d else 3, dx], second_in.at[chunk, 1, 1 - d, dx],
                main_send, base + 8 + dx, second_recv.at[chunk, 1, 1 - d, 0], along(1, 2 * d - 1),
            )

    def wait_for(buffer, sem):
        pltpu.make_async_remote_copy(
            src_ref=buffer, dst_ref=buffer, send_sem=own_sem, recv_sem=sem,
            device_id=along(0, 1), device_id_type=MESH,
        ).wait_recv()

    def pass_on(chunk):
        for way in range(2):
            for d in range(2):
                dp, half = (1, 0) if d == 0 else (3, 2)
                wait_for(first_in.at[chunk, way, d], first_recv.at[chunk, way, d])
                part[chunk, way, dp, half : half + 2] = (
                    to_f32(part[chunk, way, dp, half : half + 2]) + to_f32(first_in[chunk, way, d])
                ).astype(BF16)
                send(
                    part.at[chunk, way, dp, pl.ds(half, 2)],
                    second_in.at[chunk, way, d, pl.ds(half, 2)],
                    main_send, chunk * 16 + 12 + 2 * way + d,
                    second_recv.at[chunk, way, d, 1], along(way, 1 - 2 * d),
                )

    def turn_corner(chunk):
        for way in range(2):
            for d in range(2):
                for late in range(2):
                    half = 2 * ((1 - late + d) % 2)
                    wait_for(
                        second_in.at[chunk, way, d, pl.ds(half, 2)],
                        second_recv.at[chunk, way, d, late],
                    )
            for ds in (2, 1, 3, 0):
                total = (
                    to_f32(part[chunk, way, 0, ds])
                    + to_f32(second_in[chunk, way, 0, ds])
                    + to_f32(second_in[chunk, way, 1, ds])
                ).astype(BF16)
                mid[chunk, way, ds, 0] = total[:, :16]
                mid[chunk, way, ds, 1] = total[:, 16:]
                base = chunk * 12 + way * 6
                axis = 1 - way
                if ds == 2:
                    for d in range(2):
                        send(
                            mid.at[chunk, way, 2, d], third_in.at[chunk, way, d],
                            side_send, base + d, third_recv.at[chunk, way, d],
                            along(axis, 1 - 2 * d),
                        )
                if ds in (1, 3):
                    d, h = (0, 1) if ds == 1 else (1, 0)
                    send(
                        mid.at[chunk, way, ds, h], fourth_in.at[chunk, way, d, h],
                        side_send, base + 2 + d, fourth_recv.at[chunk, way, d, h],
                        along(axis, 1 - 2 * d),
                    )

    def pass_on_side(chunk):
        for way in range(2):
            for d in range(2):
                ds = 1 if d == 0 else 3
                wait_for(third_in.at[chunk, way, d], third_recv.at[chunk, way, d])
                mid[chunk, way, ds, d] = (
                    to_f32(mid[chunk, way, ds, d]) + to_f32(third_in[chunk, way, d])
                ).astype(BF16)
                send(
                    mid.at[chunk, way, ds, d], fourth_in.at[chunk, way, d, d],
                    side_send, chunk * 12 + way * 6 + 4 + d, fourth_recv.at[chunk, way, d, d],
                    along(1 - way, 1 - 2 * d),
                )

    def spread(chunk):
        for way in range(2):
            for d in range(2):
                for h in range(2):
                    wait_for(fourth_in.at[chunk, way, d, h], fourth_recv.at[chunk, way, d, h])
            for h in range(2):
                place = 2 * way + h
                base = pl.multiple_of(target_group(chunk, place) * GROUP, GROUP)
                for j in range(J_LOCAL):
                    total = (
                        to_f32(mid[chunk, way, 0, h, j])
                        + to_f32(fourth_in[chunk, way, 0, h, j])
                        + to_f32(fourth_in[chunk, way, 1, h, j])
                    )
                    total = jnp.where(lane < count_of(rep * J_LOCAL + j), total, 0.0)
                    blocks[pl.ds(base, GROUP), j, :, :] = total.astype(BF16).reshape(GROUP, 2, SLOTS)
                near = CHUNKS[chunk][place] == 0
                inside = wide - group * GROUP

                def push(step, carry, base=base, near=near):
                    peer = base + (lax.rem(inside + step, GROUP) if near else step)
                    pltpu.make_async_remote_copy(
                        src_ref=blocks.at[peer],
                        dst_ref=blocks_in.at[wide],
                        send_sem=spread_send,
                        recv_sem=spread_recv.at[chunk],
                        device_id={"wide": peer, "rep": rep},
                        device_id_type=MESH,
                    ).start()
                    return carry

                lax.fori_loop(1 if near else 0, GROUP, push, 0)

    def blocks_copy(many, sem):
        return pltpu.make_async_remote_copy(
            src_ref=blocks.at[pl.ds(0, many)],
            dst_ref=blocks_in.at[pl.ds(0, many)],
            send_sem=spread_send,
            recv_sem=sem,
            device_id=along(0, 1),
            device_id_type=MESH,
        )

    def assemble(chunk):
        blocks_copy(32 - chunk, spread_recv.at[chunk]).wait_recv()
        row_count = count_of(wide)
        for away in CHUNKS[chunk]:
            source = lax.rem(group - away + GROUP, GROUP)
            at = pl.multiple_of(source * GROUP, GROUP)
            to = pl.multiple_of(source * 16, 16)
            for j in range(J_LOCAL):
                block = blocks_in[pl.ds(at, GROUP), j, :, :].reshape(16, SLOTS)
                out_ref[j, pl.ds(to, 16), :] = jnp.where(
                    row + to < row_count, to_f32(block), 0.0
                ).astype(BF16)

    amps_load.wait()
    gather_rows(0)
    gather_rows(1)
    pl.semaphore_wait(barrier, WIDE - 1 + 4)
    multiply(0)
    pass_on(0)
    multiply(1)
    turn_corner(0)
    pass_on(1)
    pass_on_side(0)
    spread(0)
    turn_corner(1)
    pass_on_side(1)
    spread(1)
    own = pltpu.make_async_copy(blocks.at[wide], blocks_in.at[wide], own_sem)
    own.start()
    assemble(0)
    own.wait()
    assemble(1)

    blocks_copy(WIDE - 1, spread_recv.at[0]).wait_send()
    for copy in sent:
        copy.wait_send()


def body(amplitudes, integrals, occ_irrep, vir_count):
    dma = pltpu.SemaphoreType.DMA
    out = pl.pallas_call(
        kernel,
        out_shape=jax.ShapeDtypeStruct((J_LOCAL, SLOTS, SLOTS), BF16),
        in_specs=[pl.BlockSpec(memory_space=pltpu.HBM)] * 4,
        out_specs=pl.BlockSpec(memory_space=pltpu.VMEM),
        scratch_shapes=[
            pltpu.SMEM((80,), jnp.int32),
            pltpu.SMEM((8,), jnp.int32),
            pltpu.VMEM((WIDE, K_LOCAL, 2, SLOTS), BF16),
            pltpu.VMEM((WIDE, J_LOCAL, 2, SLOTS), BF16),
            pltpu.VMEM((WIDE, K_LOCAL, 2, SLOTS), BF16),
            pltpu.VMEM((K_LOCAL, SLOTS, 80, SLOTS), BF16),
            pltpu.VMEM((80, K_LOCAL * SLOTS, SLOTS), BF16),
            pltpu.VMEM((2, 64, K_LOCAL * SLOTS), BF16),
            pltpu.VMEM((2, 2, 4, 4, J_LOCAL, 32, SLOTS), BF16),
            pltpu.VMEM((2, 2, 2, 2, J_LOCAL, 32, SLOTS), BF16),
            pltpu.VMEM((2, 2, 2, 4, J_LOCAL, 32, SLOTS), BF16),
            pltpu.VMEM((2, 2, 4, 2, J_LOCAL, 16, SLOTS), BF16),
            pltpu.VMEM((2, 2, 2, J_LOCAL, 16, SLOTS), BF16),
            pltpu.VMEM((2, 2, 2, 2, J_LOCAL, 16, SLOTS), BF16),
            dma((K_LOCAL + 3,)),
            dma,
            dma,
            dma((2,)),
            dma((32,)),
            dma((2, 2, 2)),
            dma((2, 2, 2, 2)),
            dma((24,)),
            dma((2, 2, 2)),
            dma((2, 2, 2, 2)),
        ],
        compiler_params=pltpu.CompilerParams(
            collective_id=0, has_side_effects=True, vmem_limit_bytes=63 * 2**20
        ),
        cost_estimate=pl.CostEstimate(
            flops=2 * 128 * 640 * 10240, bytes_accessed=14 * 2**20, transcendentals=0
        ),
    )(amplitudes, integrals, occ_irrep, vir_count)
    return out.transpose(1, 0, 2)[None]


def solution(mesh):
    in_specs = (P(None, "rep", "wide", None), P("rep", None, None, None), P(), P())
    out_specs = P("wide", None, "rep", None)
    return jax.shard_map(body, mesh=mesh, in_specs=in_specs, out_specs=out_specs, check_vma=False)
```

```python
import jax
import jax.numpy as jnp
from jax import lax
from jax.experimental import pallas as pl
from jax.experimental.pallas import tpu as pltpu
from jax.sharding import PartitionSpec as P

SYM = 3
MESH = pl.DeviceIdType.MESH
F32 = jnp.float32
BF16 = jnp.bfloat16

WIDE = 64
GROUP = 8
SLOTS = 128
SIDE = 4
K_LOCAL = 5
J_LOCAL = 5
SLABS = 5
ORDER = (2, 3, 1, 0)
CHUNKS = ((3, -3, 4, -2), (2, -1, 1, 0))


def to_f32(value):
    return value.astype(F32)


def kernel(
    amps_hbm, ints_hbm, occ_hbm, vir_hbm, blocks_in,
    occ_ref, vir_ref, amps, blocks, raw, weights, rows, part, first_in, second_in, mid, third_in, fourth_in,
    load_sems, own_sem, spread_send, spread_recv, main_send, first_recv, second_recv,
    side_send, third_recv, fourth_recv,
):
    wide = lax.axis_index("wide")
    rep = lax.axis_index("rep")
    x, y = rep // SIDE, rep % SIDE
    group = wide // GROUP

    amps_load = pltpu.make_async_copy(amps_hbm, amps, load_sems.at[K_LOCAL])
    amps_load.start()
    label_loads = [
        pltpu.make_async_copy(occ_hbm, occ_ref, load_sems.at[K_LOCAL + 1]),
        pltpu.make_async_copy(vir_hbm, vir_ref, load_sems.at[K_LOCAL + 2]),
    ]
    for load in label_loads:
        load.start()
    first_target = lax.rem(x + ORDER[0], SIDE)
    slab = [lax.rem(first_target + n, SLABS) for n in range(SLABS)]
    int_loads = [
        pltpu.make_async_copy(
            ints_hbm.at[:, :, pl.ds(pl.multiple_of(slab[n] * 16, 16), 16), :],
            raw.at[n],
            load_sems.at[n],
        )
        for n in range(SLABS)
    ]
    for load in int_loads:
        load.start()

    def along(axis, step):
        if axis == 0:
            other = lax.rem(x + step + SIDE, SIDE) * SIDE + y
        else:
            other = x * SIDE + lax.rem(y + step + SIDE, SIDE)
        return {"wide": wide, "rep": other}

    barrier = pltpu.get_barrier_semaphore()

    def greet(step, carry):
        peer = lax.rem(wide + WIDE // 2 + (1 - 2 * (step % 2)) * (step // 2) + WIDE, WIDE)
        pl.semaphore_signal(
            barrier, inc=1, device_id={"wide": peer, "rep": rep}, device_id_type=MESH
        )
        return carry

    for axis in range(2):
        for step in (1, -1):
            pl.semaphore_signal(
                barrier, inc=1, device_id=along(axis, step), device_id_type=MESH
            )
    lax.fori_loop(1, WIDE, greet, 0)
    def turn_slab(n):
        int_loads[n].wait()
        j = slab[n] * 16

        def turn(step, carry):
            c = pl.multiple_of(step * 16, 16)
            for k in range(K_LOCAL):
                to = pl.multiple_of(k * SLOTS + step * 16, 16)
                weights[pl.ds(j, 16), pl.ds(to, 16), :] = jnp.swapaxes(
                    raw[n, k, pl.ds(c, 16), :, :], 0, 1
                )
            return carry

        lax.fori_loop(0, SLOTS // 16, turn, 0)

    for load in label_loads:
        load.wait()
    lane = lax.broadcasted_iota(jnp.int32, (16, SLOTS), 1)
    row = lax.broadcasted_iota(jnp.int32, (16, SLOTS), 0)

    def count_of(orbital):
        return vir_ref[jnp.bitwise_xor(occ_ref[orbital], SYM)]

    def target_group(chunk, place):
        return lax.rem(group + CHUNKS[chunk][place] + GROUP, GROUP)

    def gather_rows(chunk):
        for k in range(K_LOCAL):
            valid = lane < count_of(rep * K_LOCAL + k)
            for place in range(4):
                at = pl.multiple_of(target_group(chunk, place) * GROUP, GROUP)
                block = amps[pl.ds(at, GROUP), k, :, :].reshape(16, SLOTS)
                at = chunk * 64 + place * 16
                rows[at : at + 16, SLOTS * k : SLOTS * k + SLOTS] = jnp.where(
                    valid, to_f32(block), 0.0
                ).astype(BF16)

    sent = []

    def send(src, dst, sems, index, recv, device):
        copy = pltpu.make_async_remote_copy(
            src_ref=src,
            dst_ref=dst,
            send_sem=sems.at[index],
            recv_sem=recv,
            device_id=device,
            device_id_type=MESH,
        )
        copy.start()
        sent.append(copy)
        return copy

    def multiply(dx):
        def pair(t, carry):
            pieces = []
            ways = (2 + t, 1 - t)
            for dy in ways:
                target = lax.rem(x + dx, SIDE) * SIDE + lax.rem(y + dy, SIDE)
                pieces += [weights[target * J_LOCAL + j] for j in range(J_LOCAL)]
            product = jnp.dot(
                rows[...], jnp.concatenate(pieces, axis=1), preferred_element_type=F32
            ).astype(BF16)
            for n, dy in enumerate(ways):
                for j in range(J_LOCAL):
                    at = (n * J_LOCAL + j) * SLOTS
                    for chunk in range(2):
                        top = chunk * 64
                        part[chunk, 0, dx, dy, j] = product[top : top + 32, at : at + SLOTS]
                        part[chunk, 1, dy, dx, j] = product[top + 32 : top + 64, at : at + SLOTS]
            return carry

        lax.fori_loop(0, 2, pair, 0)

    def send_parts(chunk, dx):
        base = chunk * 16
        if dx == 2:
            for d, half in ((0, 0), (1, 2)):
                send(
                    part.at[chunk, 0, 2, pl.ds(half, 2)], first_in.at[chunk, 0, d],
                    main_send, base + d, first_recv.at[chunk, 0, d], along(0, 1 - 2 * d),
                )
        if dx in (1, 3):
            d, half = (0, 2) if dx == 1 else (1, 0)
            send(
                part.at[chunk, 0, dx, pl.ds(half, 2)],
                second_in.at[chunk, 0, d, pl.ds(half, 2)],
                main_send, base + 2 + d, second_recv.at[chunk, 0, d, 0], along(0, 1 - 2 * d),
            )
        d = 0 if dx < 2 else 1
        send(
            part.at[chunk, 1, 2, dx], first_in.at[chunk, 1, d, dx % 2],
            main_send, base + 4 + dx, first_recv.at[chunk, 1, d], along(1, 1 - 2 * d),
        )
        send(
            part.at[chunk, 1, 1 if d else 3, dx], second_in.at[chunk, 1, 1 - d, dx],
            main_send, base + 8 + dx, second_recv.at[chunk, 1, 1 - d, 0], along(1, 2 * d - 1),
        )

    def wait_for(buffer, sem):
        pltpu.make_async_remote_copy(
            src_ref=buffer, dst_ref=buffer, send_sem=own_sem, recv_sem=sem,
            device_id=along(0, 1), device_id_type=MESH,
        ).wait_recv()

    def pass_on(chunk):
        for way in range(2):
            for d in range(2):
                dp, half = (1, 0) if d == 0 else (3, 2)
                wait_for(first_in.at[chunk, way, d], first_recv.at[chunk, way, d])
                part[chunk, way, dp, half : half + 2] = (
                    to_f32(part[chunk, way, dp, half : half + 2]) + to_f32(first_in[chunk, way, d])
                ).astype(BF16)
                send(
                    part.at[chunk, way, dp, pl.ds(half, 2)],
                    second_in.at[chunk, way, d, pl.ds(half, 2)],
                    main_send, chunk * 16 + 12 + 2 * way + d,
                    second_recv.at[chunk, way, d, 1], along(way, 1 - 2 * d),
                )

    def turn_corner(chunk):
        for way in range(2):
            for d in range(2):
                for late in range(2):
                    half = 2 * ((1 - late + d) % 2)
                    wait_for(
                        second_in.at[chunk, way, d, pl.ds(half, 2)],
                        second_recv.at[chunk, way, d, late],
                    )
            for ds in (2, 1, 3, 0):
                total = (
                    to_f32(part[chunk, way, 0, ds])
                    + to_f32(second_in[chunk, way, 0, ds])
                    + to_f32(second_in[chunk, way, 1, ds])
                ).astype(BF16)
                mid[chunk, way, ds, 0] = total[:, :16]
                mid[chunk, way, ds, 1] = total[:, 16:]
                base = chunk * 12 + way * 6
                axis = 1 - way
                if ds == 2:
                    for d in range(2):
                        send(
                            mid.at[chunk, way, 2, d], third_in.at[chunk, way, d],
                            side_send, base + d, third_recv.at[chunk, way, d],
                            along(axis, 1 - 2 * d),
                        )
                if ds in (1, 3):
                    d, h = (0, 1) if ds == 1 else (1, 0)
                    send(
                        mid.at[chunk, way, ds, h], fourth_in.at[chunk, way, d, h],
                        side_send, base + 2 + d, fourth_recv.at[chunk, way, d, h],
                        along(axis, 1 - 2 * d),
                    )

    def pass_on_side(chunk):
        for way in range(2):
            for d in range(2):
                ds = 1 if d == 0 else 3
                wait_for(third_in.at[chunk, way, d], third_recv.at[chunk, way, d])
                mid[chunk, way, ds, d] = (
                    to_f32(mid[chunk, way, ds, d]) + to_f32(third_in[chunk, way, d])
                ).astype(BF16)
                send(
                    mid.at[chunk, way, ds, d], fourth_in.at[chunk, way, d, d],
                    side_send, chunk * 12 + way * 6 + 4 + d, fourth_recv.at[chunk, way, d, d],
                    along(1 - way, 1 - 2 * d),
                )

    def spread(chunk):
        for way in range(2):
            for d in range(2):
                for h in range(2):
                    wait_for(fourth_in.at[chunk, way, d, h], fourth_recv.at[chunk, way, d, h])
            bases, own_group = [], []
            for h in range(2):
                place = 2 * way + h
                base = pl.multiple_of(target_group(chunk, place) * GROUP, GROUP)
                bases.append(base)
                own_group.append(CHUNKS[chunk][place] == 0)
                row_count = jnp.zeros_like(row)
                for n in range(GROUP):
                    row_count = jnp.where(row >> 1 == n, count_of(base + n), row_count)
                row_valid = 2 * wide + (row & 1) < row_count
                for j in range(J_LOCAL):
                    total = (
                        to_f32(mid[chunk, way, 0, h, j])
                        + to_f32(fourth_in[chunk, way, 0, h, j])
                        + to_f32(fourth_in[chunk, way, 1, h, j])
                    )
                    valid = row_valid & (lane < count_of(rep * J_LOCAL + j))
                    total = jnp.where(valid, total, 0.0).astype(BF16)
                    blocks[pl.ds(base, GROUP), j, :, :] = total.reshape(GROUP, 2, SLOTS)
            inside = wide - group * GROUP

            def push_to(peer):
                pltpu.make_async_remote_copy(
                    src_ref=blocks.at[peer],
                    dst_ref=blocks_in.at[wide],
                    send_sem=spread_send,
                    recv_sem=spread_recv.at[chunk],
                    device_id={"wide": peer, "rep": rep},
                    device_id_type=MESH,
                ).start()

            def push(step, carry, bases=bases, own_group=own_group):
                for base, near in zip(bases, own_group):
                    push_to(base + (lax.rem(inside + step, GROUP) if near else step))
                return carry

            if own_group[1]:
                push_to(bases[0])
            lax.fori_loop(1 if own_group[1] else 0, GROUP, push, 0)

    def blocks_copy(many, sem):
        return pltpu.make_async_remote_copy(
            src_ref=blocks.at[pl.ds(0, many)],
            dst_ref=blocks_in.at[pl.ds(0, many)],
            send_sem=spread_send,
            recv_sem=sem,
            device_id=along(0, 1),
            device_id_type=MESH,
        )

    amps_load.wait()
    gather_rows(0)
    gather_rows(1)
    ready = 0
    for dx, needed in zip(ORDER, (2, 4, 5, 5)):
        for n in range(ready, needed):
            turn_slab(n)
        ready = needed
        multiply(dx)
        if dx == ORDER[0]:
            pl.semaphore_wait(barrier, WIDE - 1 + 4)
        send_parts(0, dx)
    pass_on(0)
    for dx in ORDER:
        send_parts(1, dx)
    turn_corner(0)
    pass_on(1)
    pass_on_side(0)
    spread(0)
    turn_corner(1)
    pass_on_side(1)
    spread(1)
    own = pltpu.make_async_copy(blocks.at[wide], blocks_in.at[wide], own_sem)
    own.start()
    own.wait()
    for copy in sent:
        copy.wait_send()
    blocks_copy(WIDE - 1, spread_recv.at[0]).wait_send()
    blocks_copy(WIDE // 2, spread_recv.at[0]).wait_recv()
    blocks_copy(WIDE // 2 - 1, spread_recv.at[1]).wait_recv()


def body(amplitudes, integrals, occ_irrep, vir_count):
    dma = pltpu.SemaphoreType.DMA
    out = pl.pallas_call(
        kernel,
        out_shape=jax.ShapeDtypeStruct((WIDE, J_LOCAL, 2, SLOTS), BF16),
        in_specs=[pl.BlockSpec(memory_space=pltpu.HBM)] * 4,
        out_specs=pl.BlockSpec(memory_space=pl.ANY),
        scratch_shapes=[
            pltpu.SMEM((80,), jnp.int32),
            pltpu.SMEM((8,), jnp.int32),
            pltpu.VMEM((WIDE, K_LOCAL, 2, SLOTS), BF16),
            pltpu.VMEM((WIDE, J_LOCAL, 2, SLOTS), BF16),
            pltpu.VMEM((SLABS, K_LOCAL, SLOTS, 16, SLOTS), BF16),
            pltpu.VMEM((80, K_LOCAL * SLOTS, SLOTS), BF16),
            pltpu.VMEM((128, K_LOCAL * SLOTS), BF16),
            pltpu.VMEM((2, 2, 4, 4, J_LOCAL, 32, SLOTS), BF16),
            pltpu.VMEM((2, 2, 2, 2, J_LOCAL, 32, SLOTS), BF16),
            pltpu.VMEM((2, 2, 2, 4, J_LOCAL, 32, SLOTS), BF16),
            pltpu.VMEM((2, 2, 4, 2, J_LOCAL, 16, SLOTS), BF16),
            pltpu.VMEM((2, 2, 2, J_LOCAL, 16, SLOTS), BF16),
            pltpu.VMEM((2, 2, 2, 2, J_LOCAL, 16, SLOTS), BF16),
            dma((K_LOCAL + 3,)),
            dma,
            dma,
            dma((2,)),
            dma((32,)),
            dma((2, 2, 2)),
            dma((2, 2, 2, 2)),
            dma((24,)),
            dma((2, 2, 2)),
            dma((2, 2, 2, 2)),
        ],
        compiler_params=pltpu.CompilerParams(
            collective_id=0, has_side_effects=True, vmem_limit_bytes=63 * 2**20
        ),
        cost_estimate=pl.CostEstimate(
            flops=2 * 128 * 640 * 10240, bytes_accessed=14 * 2**20, transcendentals=0
        ),
    )(amplitudes, integrals, occ_irrep, vir_count)
    return out.transpose(0, 2, 1, 3).reshape(1, 2 * WIDE, J_LOCAL, SLOTS)


def solution(mesh):
    in_specs = (P(None, "rep", "wide", None), P("rep", None, None, None), P(), P())
    out_specs = P("wide", None, "rep", None)
    return jax.shard_map(body, mesh=mesh, in_specs=in_specs, out_specs=out_specs, check_vma=False)
```

```python
import jax
import jax.numpy as jnp
from jax import lax
from jax.experimental import pallas as pl
from jax.experimental.pallas import tpu as pltpu
from jax.sharding import PartitionSpec as P

SYM = 3
MESH = pl.DeviceIdType.MESH
F32 = jnp.float32
BF16 = jnp.bfloat16

WIDE = 64
GROUP = 8
SLOTS = 128
SIDE = 4
K_LOCAL = 5
J_LOCAL = 5
SLABS = 5
ORDER = (2, 3, 1, 0)
CHUNKS = ((3, -3, 4, -2), (2, -1, 1, 0))


def to_f32(value):
    return value.astype(F32)


def kernel(
    amps_hbm, ints_hbm, occ_hbm, vir_hbm, blocks_in,
    occ_ref, vir_ref, amps, blocks, raw, weights, rows, part, first_in, second_in, mid, third_in, fourth_in,
    load_sems, own_sem, spread_send, spread_recv, main_send, first_recv, second_recv,
    side_send, third_recv, fourth_recv, relay_one, relay_two,
):
    wide = lax.axis_index("wide")
    rep = lax.axis_index("rep")
    x, y = rep // SIDE, rep % SIDE
    group = wide // GROUP

    amps_load = pltpu.make_async_copy(amps_hbm, amps, load_sems.at[K_LOCAL])
    amps_load.start()
    label_loads = [
        pltpu.make_async_copy(occ_hbm, occ_ref, load_sems.at[K_LOCAL + 1]),
        pltpu.make_async_copy(vir_hbm, vir_ref, load_sems.at[K_LOCAL + 2]),
    ]
    for load in label_loads:
        load.start()
    first_target = lax.rem(x + ORDER[0], SIDE)
    slab = [lax.rem(first_target + n, SLABS) for n in range(SLABS)]
    int_loads = [
        pltpu.make_async_copy(
            ints_hbm.at[:, :, pl.ds(pl.multiple_of(slab[n] * 16, 16), 16), :],
            raw.at[n],
            load_sems.at[n],
        )
        for n in range(SLABS)
    ]
    for load in int_loads:
        load.start()

    def along(axis, step):
        if axis == 0:
            other = lax.rem(x + step + SIDE, SIDE) * SIDE + y
        else:
            other = x * SIDE + lax.rem(y + step + SIDE, SIDE)
        return {"wide": wide, "rep": other}

    barrier = pltpu.get_barrier_semaphore()
    inside = wide - group * GROUP

    def greet(step, carry):
        place = lax.rem(GROUP + inside + step, 3 * GROUP)
        peer = lax.rem(group * GROUP + place - GROUP + WIDE, WIDE)
        pl.semaphore_signal(
            barrier, inc=1, device_id={"wide": peer, "rep": rep}, device_id_type=MESH
        )
        return carry

    def tell(relay, groups):
        for away in (groups, -groups):
            peer = lax.rem(wide + away * GROUP + WIDE, WIDE)
            pl.semaphore_signal(
                relay, inc=1, device_id={"wide": peer, "rep": rep}, device_id_type=MESH
            )

    for axis in range(2):
        for step in (1, -1):
            pl.semaphore_signal(
                barrier, inc=1, device_id=along(axis, step), device_id_type=MESH
            )
    lax.fori_loop(1, 3 * GROUP, greet, 0)
    pl.semaphore_wait(barrier, 3 * GROUP - 1 + 4)
    tell(relay_one, 1)

    def turn_slab(n):
        int_loads[n].wait()
        j = slab[n] * 16

        def turn(step, carry):
            c = pl.multiple_of(step * 16, 16)
            for k in range(K_LOCAL):
                to = pl.multiple_of(k * SLOTS + step * 16, 16)
                weights[pl.ds(j, 16), pl.ds(to, 16), :] = jnp.swapaxes(
                    raw[n, k, pl.ds(c, 16), :, :], 0, 1
                )
            return carry

        lax.fori_loop(0, SLOTS // 16, turn, 0)

    for load in label_loads:
        load.wait()
    lane = lax.broadcasted_iota(jnp.int32, (16, SLOTS), 1)
    row = lax.broadcasted_iota(jnp.int32, (16, SLOTS), 0)

    def count_of(orbital):
        return vir_ref[jnp.bitwise_xor(occ_ref[orbital], SYM)]

    def target_group(chunk, place):
        return lax.rem(group + CHUNKS[chunk][place] + GROUP, GROUP)

    def gather_rows(chunk):
        for k in range(K_LOCAL):
            valid = lane < count_of(rep * K_LOCAL + k)
            for place in range(4):
                at = pl.multiple_of(target_group(chunk, place) * GROUP, GROUP)
                block = amps[pl.ds(at, GROUP), k, :, :].reshape(16, SLOTS)
                at = chunk * 64 + place * 16
                rows[at : at + 16, SLOTS * k : SLOTS * k + SLOTS] = jnp.where(
                    valid, to_f32(block), 0.0
                ).astype(BF16)

    sent = []

    def send(src, dst, sems, index, recv, device):
        copy = pltpu.make_async_remote_copy(
            src_ref=src,
            dst_ref=dst,
            send_sem=sems.at[index],
            recv_sem=recv,
            device_id=device,
            device_id_type=MESH,
        )
        copy.start()
        sent.append(copy)
        return copy

    def multiply(dx):
        def pair(t, carry):
            pieces = []
            ways = (2 + t, 1 - t)
            for dy in ways:
                target = lax.rem(x + dx, SIDE) * SIDE + lax.rem(y + dy, SIDE)
                pieces += [weights[target * J_LOCAL + j] for j in range(J_LOCAL)]
            product = jnp.dot(
                rows[...], jnp.concatenate(pieces, axis=1), preferred_element_type=F32
            ).astype(BF16)
            for n, dy in enumerate(ways):
                for j in range(J_LOCAL):
                    at = (n * J_LOCAL + j) * SLOTS
                    for chunk in range(2):
                        top = chunk * 64
                        part[chunk, 0, dx, dy, j] = product[top : top + 32, at : at + SLOTS]
                        part[chunk, 1, dy, dx, j] = product[top + 32 : top + 64, at : at + SLOTS]
            return carry

        lax.fori_loop(0, 2, pair, 0)

    def send_parts(chunk, dx):
        base = chunk * 16
        if dx == 2:
            for d, half in ((0, 0), (1, 2)):
                send(
                    part.at[chunk, 0, 2, pl.ds(half, 2)], first_in.at[chunk, 0, d],
                    main_send, base + d, first_recv.at[chunk, 0, d], along(0, 1 - 2 * d),
                )
        if dx in (1, 3):
            d, half = (0, 2) if dx == 1 else (1, 0)
            send(
                part.at[chunk, 0, dx, pl.ds(half, 2)],
                second_in.at[chunk, 0, d, pl.ds(half, 2)],
                main_send, base + 2 + d, second_recv.at[chunk, 0, d, 0], along(0, 1 - 2 * d),
            )
        d = 0 if dx < 2 else 1
        send(
            part.at[chunk, 1, 2, dx], first_in.at[chunk, 1, d, dx % 2],
            main_send, base + 4 + dx, first_recv.at[chunk, 1, d], along(1, 1 - 2 * d),
        )
        send(
            part.at[chunk, 1, 1 if d else 3, dx], second_in.at[chunk, 1, 1 - d, dx],
            main_send, base + 8 + dx, second_recv.at[chunk, 1, 1 - d, 0], along(1, 2 * d - 1),
        )

    def wait_for(buffer, sem):
        pltpu.make_async_remote_copy(
            src_ref=buffer, dst_ref=buffer, send_sem=own_sem, recv_sem=sem,
            device_id=along(0, 1), device_id_type=MESH,
        ).wait_recv()

    def pass_on(chunk):
        for way in range(2):
            for d in range(2):
                dp, half = (1, 0) if d == 0 else (3, 2)
                wait_for(first_in.at[chunk, way, d], first_recv.at[chunk, way, d])
                part[chunk, way, dp, half : half + 2] = (
                    to_f32(part[chunk, way, dp, half : half + 2]) + to_f32(first_in[chunk, way, d])
                ).astype(BF16)
                send(
                    part.at[chunk, way, dp, pl.ds(half, 2)],
                    second_in.at[chunk, way, d, pl.ds(half, 2)],
                    main_send, chunk * 16 + 12 + 2 * way + d,
                    second_recv.at[chunk, way, d, 1], along(way, 1 - 2 * d),
                )

    def turn_corner(chunk):
        for way in range(2):
            for d in range(2):
                for late in range(2):
                    half = 2 * ((1 - late + d) % 2)
                    wait_for(
                        second_in.at[chunk, way, d, pl.ds(half, 2)],
                        second_recv.at[chunk, way, d, late],
                    )
            for ds in (2, 1, 3, 0):
                total = (
                    to_f32(part[chunk, way, 0, ds])
                    + to_f32(second_in[chunk, way, 0, ds])
                    + to_f32(second_in[chunk, way, 1, ds])
                ).astype(BF16)
                mid[chunk, way, ds, 0] = total[:, :16]
                mid[chunk, way, ds, 1] = total[:, 16:]
                base = chunk * 12 + way * 6
                axis = 1 - way
                if ds == 2:
                    for d in range(2):
                        send(
                            mid.at[chunk, way, 2, d], third_in.at[chunk, way, d],
                            side_send, base + d, third_recv.at[chunk, way, d],
                            along(axis, 1 - 2 * d),
                        )
                if ds in (1, 3):
                    d, h = (0, 1) if ds == 1 else (1, 0)
                    send(
                        mid.at[chunk, way, ds, h], fourth_in.at[chunk, way, d, h],
                        side_send, base + 2 + d, fourth_recv.at[chunk, way, d, h],
                        along(axis, 1 - 2 * d),
                    )

    def pass_on_side(chunk):
        for way in range(2):
            for d in range(2):
                ds = 1 if d == 0 else 3
                wait_for(third_in.at[chunk, way, d], third_recv.at[chunk, way, d])
                mid[chunk, way, ds, d] = (
                    to_f32(mid[chunk, way, ds, d]) + to_f32(third_in[chunk, way, d])
                ).astype(BF16)
                send(
                    mid.at[chunk, way, ds, d], fourth_in.at[chunk, way, d, d],
                    side_send, chunk * 12 + way * 6 + 4 + d, fourth_recv.at[chunk, way, d, d],
                    along(1 - way, 1 - 2 * d),
                )

    def spread(chunk):
        for way in range(2):
            for d in range(2):
                for h in range(2):
                    wait_for(fourth_in.at[chunk, way, d, h], fourth_recv.at[chunk, way, d, h])
            bases, own_group = [], []
            for h in range(2):
                place = 2 * way + h
                base = pl.multiple_of(target_group(chunk, place) * GROUP, GROUP)
                bases.append(base)
                own_group.append(CHUNKS[chunk][place] == 0)
                row_count = jnp.zeros_like(row)
                for n in range(GROUP):
                    row_count = jnp.where(row >> 1 == n, count_of(base + n), row_count)
                row_valid = 2 * wide + (row & 1) < row_count
                for j in range(J_LOCAL):
                    total = (
                        to_f32(mid[chunk, way, 0, h, j])
                        + to_f32(fourth_in[chunk, way, 0, h, j])
                        + to_f32(fourth_in[chunk, way, 1, h, j])
                    )
                    valid = row_valid & (lane < count_of(rep * J_LOCAL + j))
                    total = jnp.where(valid, total, 0.0).astype(BF16)
                    blocks[pl.ds(base, GROUP), j, :, :] = total.reshape(GROUP, 2, SLOTS)

            def push_to(peer):
                pltpu.make_async_remote_copy(
                    src_ref=blocks.at[peer],
                    dst_ref=blocks_in.at[wide],
                    send_sem=spread_send,
                    recv_sem=spread_recv.at[chunk],
                    device_id={"wide": peer, "rep": rep},
                    device_id_type=MESH,
                ).start()

            def push(step, carry, bases=bases, own_group=own_group):
                for base, near in zip(bases, own_group):
                    push_to(base + (lax.rem(inside + step, GROUP) if near else step))
                return carry

            if own_group[1]:
                push_to(bases[0])
            lax.fori_loop(1 if own_group[1] else 0, GROUP, push, 0)

    def blocks_copy(many, sem):
        return pltpu.make_async_remote_copy(
            src_ref=blocks.at[pl.ds(0, many)],
            dst_ref=blocks_in.at[pl.ds(0, many)],
            send_sem=spread_send,
            recv_sem=sem,
            device_id=along(0, 1),
            device_id_type=MESH,
        )

    amps_load.wait()
    gather_rows(0)
    gather_rows(1)
    ready = 0
    for dx, needed in zip(ORDER, (2, 4, 5, 5)):
        for n in range(ready, needed):
            turn_slab(n)
        ready = needed
        multiply(dx)
        send_parts(0, dx)
        if dx == ORDER[0]:
            pl.semaphore_wait(relay_one, 2)
            tell(relay_two, 2)
    pass_on(0)
    for dx in ORDER:
        send_parts(1, dx)
    turn_corner(0)
    pass_on(1)
    pass_on_side(0)
    pl.semaphore_wait(relay_two, 2)
    spread(0)
    turn_corner(1)
    pass_on_side(1)
    spread(1)
    own = pltpu.make_async_copy(blocks.at[wide], blocks_in.at[wide], own_sem)
    own.start()
    own.wait()
    for copy in sent:
        copy.wait_send()
    blocks_copy(WIDE - 1, spread_recv.at[0]).wait_send()
    blocks_copy(WIDE // 2, spread_recv.at[0]).wait_recv()
    blocks_copy(WIDE // 2 - 1, spread_recv.at[1]).wait_recv()


def body(amplitudes, integrals, occ_irrep, vir_count):
    dma = pltpu.SemaphoreType.DMA
    out = pl.pallas_call(
        kernel,
        out_shape=jax.ShapeDtypeStruct((WIDE, J_LOCAL, 2, SLOTS), BF16),
        in_specs=[pl.BlockSpec(memory_space=pltpu.HBM)] * 4,
        out_specs=pl.BlockSpec(memory_space=pl.ANY),
        scratch_shapes=[
            pltpu.SMEM((80,), jnp.int32),
            pltpu.SMEM((8,), jnp.int32),
            pltpu.VMEM((WIDE, K_LOCAL, 2, SLOTS), BF16),
            pltpu.VMEM((WIDE, J_LOCAL, 2, SLOTS), BF16),
            pltpu.VMEM((SLABS, K_LOCAL, SLOTS, 16, SLOTS), BF16),
            pltpu.VMEM((80, K_LOCAL * SLOTS, SLOTS), BF16),
            pltpu.VMEM((128, K_LOCAL * SLOTS), BF16),
            pltpu.VMEM((2, 2, 4, 4, J_LOCAL, 32, SLOTS), BF16),
            pltpu.VMEM((2, 2, 2, 2, J_LOCAL, 32, SLOTS), BF16),
            pltpu.VMEM((2, 2, 2, 4, J_LOCAL, 32, SLOTS), BF16),
            pltpu.VMEM((2, 2, 4, 2, J_LOCAL, 16, SLOTS), BF16),
            pltpu.VMEM((2, 2, 2, J_LOCAL, 16, SLOTS), BF16),
            pltpu.VMEM((2, 2, 2, 2, J_LOCAL, 16, SLOTS), BF16),
            dma((K_LOCAL + 3,)),
            dma,
            dma,
            dma((2,)),
            dma((32,)),
            dma((2, 2, 2)),
            dma((2, 2, 2, 2)),
            dma((24,)),
            dma((2, 2, 2)),
            dma((2, 2, 2, 2)),
            pltpu.SemaphoreType.REGULAR,
            pltpu.SemaphoreType.REGULAR,
        ],
        compiler_params=pltpu.CompilerParams(
            collective_id=0, has_side_effects=True, vmem_limit_bytes=63 * 2**20
        ),
        cost_estimate=pl.CostEstimate(
            flops=2 * 128 * 640 * 10240, bytes_accessed=14 * 2**20, transcendentals=0
        ),
    )(amplitudes, integrals, occ_irrep, vir_count)
    return out.transpose(0, 2, 1, 3).reshape(1, 2 * WIDE, J_LOCAL, SLOTS)


def solution(mesh):
    in_specs = (P(None, "rep", "wide", None), P("rep", None, None, None), P(), P())
    out_specs = P("wide", None, "rep", None)
    return jax.shard_map(body, mesh=mesh, in_specs=in_specs, out_specs=out_specs, check_vma=False)
```

```python
import jax
import jax.numpy as jnp
from jax import lax
from jax.experimental import pallas as pl
from jax.experimental.pallas import tpu as pltpu
from jax.sharding import PartitionSpec as P

SYM = 3
MESH = pl.DeviceIdType.MESH
F32 = jnp.float32
BF16 = jnp.bfloat16

WIDE = 64
GROUP = 8
SLOTS = 128
SIDE = 4
K_LOCAL = 5
J_LOCAL = 5
SLABS = 5
ORDER = (2, 3, 1, 0)
CHUNKS = ((3, -3, 4, -2), (2, -1, 1, 0))


def to_f32(value):
    return value.astype(F32)


def kernel(
    amps_hbm, ints_hbm, occ_hbm, vir_hbm, blocks_in,
    occ_ref, vir_ref, amps, blocks, raw, weights, rows, part, first_in, second_in, mid, third_in, fourth_in,
    load_sems, own_sem, spread_send, spread_recv, main_send, first_recv, second_recv,
    side_send, third_recv, fourth_recv, relay_one, relay_two,
):
    wide = lax.axis_index("wide")
    rep = lax.axis_index("rep")
    x, y = rep // SIDE, rep % SIDE
    group = wide // GROUP

    amps_load = pltpu.make_async_copy(amps_hbm, amps, load_sems.at[K_LOCAL])
    amps_load.start()
    label_loads = [
        pltpu.make_async_copy(occ_hbm, occ_ref, load_sems.at[K_LOCAL + 1]),
        pltpu.make_async_copy(vir_hbm, vir_ref, load_sems.at[K_LOCAL + 2]),
    ]
    for load in label_loads:
        load.start()
    first_target = lax.rem(x + ORDER[0], SIDE)
    slab = [lax.rem(first_target + n, SLABS) for n in range(SLABS)]
    int_loads = [
        pltpu.make_async_copy(
            ints_hbm.at[:, :, pl.ds(pl.multiple_of(slab[n] * 16, 16), 16), :],
            raw.at[n],
            load_sems.at[n],
        )
        for n in range(SLABS)
    ]
    for load in int_loads:
        load.start()

    def along(axis, step):
        if axis == 0:
            other = lax.rem(x + step + SIDE, SIDE) * SIDE + y
        else:
            other = x * SIDE + lax.rem(y + step + SIDE, SIDE)
        return {"wide": wide, "rep": other}

    barrier = pltpu.get_barrier_semaphore()
    inside = wide - group * GROUP

    def greet(step, carry):
        place = lax.rem(GROUP + inside + step, 3 * GROUP)
        peer = lax.rem(group * GROUP + place - GROUP + WIDE, WIDE)
        pl.semaphore_signal(
            barrier, inc=1, device_id={"wide": peer, "rep": rep}, device_id_type=MESH
        )
        return carry

    def tell(relay, groups):
        for away in (groups, -groups):
            peer = lax.rem(wide + away * GROUP + WIDE, WIDE)
            pl.semaphore_signal(
                relay, inc=1, device_id={"wide": peer, "rep": rep}, device_id_type=MESH
            )

    for axis in range(2):
        for step in (1, -1):
            pl.semaphore_signal(
                barrier, inc=1, device_id=along(axis, step), device_id_type=MESH
            )
    lax.fori_loop(1, 3 * GROUP, greet, 0)
    pl.semaphore_wait(barrier, 3 * GROUP - 1 + 4)
    tell(relay_one, 1)

    def turn_slab(n):
        int_loads[n].wait()
        j = slab[n] * 16

        def turn(step, carry):
            c = pl.multiple_of(step * 16, 16)
            for k in range(K_LOCAL):
                to = pl.multiple_of(k * SLOTS + step * 16, 16)
                weights[pl.ds(j, 16), pl.ds(to, 16), :] = jnp.swapaxes(
                    raw[n, k, pl.ds(c, 16), :, :], 0, 1
                )
            return carry

        lax.fori_loop(0, SLOTS // 16, turn, 0)

    for load in label_loads:
        load.wait()
    lane = lax.broadcasted_iota(jnp.int32, (16, SLOTS), 1)
    row = lax.broadcasted_iota(jnp.int32, (16, SLOTS), 0)

    def count_of(orbital):
        return vir_ref[jnp.bitwise_xor(occ_ref[orbital], SYM)]

    def target_group(chunk, place):
        return lax.rem(group + CHUNKS[chunk][place] + GROUP, GROUP)

    def gather_rows(chunk):
        for k in range(K_LOCAL):
            valid = lane < count_of(rep * K_LOCAL + k)
            for place in range(4):
                at = pl.multiple_of(target_group(chunk, place) * GROUP, GROUP)
                block = amps[pl.ds(at, GROUP), k, :, :].reshape(16, SLOTS)
                at = chunk * 64 + place * 16
                rows[at : at + 16, SLOTS * k : SLOTS * k + SLOTS] = jnp.where(
                    valid, to_f32(block), 0.0
                ).astype(BF16)

    sent = []

    def send(src, dst, sems, index, recv, device):
        copy = pltpu.make_async_remote_copy(
            src_ref=src,
            dst_ref=dst,
            send_sem=sems.at[index],
            recv_sem=recv,
            device_id=device,
            device_id_type=MESH,
        )
        copy.start()
        sent.append(copy)
        return copy

    def multiply(dx):
        def pair(t, carry):
            pieces = []
            ways = (2 + t, 1 - t)
            for dy in ways:
                target = lax.rem(x + dx, SIDE) * SIDE + lax.rem(y + dy, SIDE)
                pieces += [weights[target * J_LOCAL + j] for j in range(J_LOCAL)]
            product = jnp.dot(
                rows[...], jnp.concatenate(pieces, axis=1), preferred_element_type=F32
            ).astype(BF16)
            for n, dy in enumerate(ways):
                for j in range(J_LOCAL):
                    at = (n * J_LOCAL + j) * SLOTS
                    for chunk in range(2):
                        top = chunk * 64
                        part[chunk, 0, dx, dy, j] = product[top : top + 32, at : at + SLOTS]
                        part[chunk, 1, dy, dx, j] = product[top + 32 : top + 64, at : at + SLOTS]
            return carry

        lax.fori_loop(0, 2, pair, 0)

    def send_parts(chunk, dx):
        base = chunk * 16
        if dx == 2:
            for d, half in ((0, 0), (1, 2)):
                send(
                    part.at[chunk, 0, 2, pl.ds(half, 2)], first_in.at[chunk, 0, d],
                    main_send, base + d, first_recv.at[chunk, 0, d], along(0, 1 - 2 * d),
                )
        if dx in (1, 3):
            d, half = (0, 2) if dx == 1 else (1, 0)
            send(
                part.at[chunk, 0, dx, pl.ds(half, 2)],
                second_in.at[chunk, 0, d, pl.ds(half, 2)],
                main_send, base + 2 + d, second_recv.at[chunk, 0, d, 0], along(0, 1 - 2 * d),
            )
        d = 0 if dx < 2 else 1
        send(
            part.at[chunk, 1, 2, dx], first_in.at[chunk, 1, d, dx % 2],
            main_send, base + 4 + dx, first_recv.at[chunk, 1, d], along(1, 1 - 2 * d),
        )
        send(
            part.at[chunk, 1, 1 if d else 3, dx], second_in.at[chunk, 1, 1 - d, dx],
            main_send, base + 8 + dx, second_recv.at[chunk, 1, 1 - d, 0], along(1, 2 * d - 1),
        )

    def wait_for(buffer, sem):
        pltpu.make_async_remote_copy(
            src_ref=buffer, dst_ref=buffer, send_sem=own_sem, recv_sem=sem,
            device_id=along(0, 1), device_id_type=MESH,
        ).wait_recv()

    def pass_on(chunk):
        for way in range(2):
            for d in range(2):
                dp, half = (1, 0) if d == 0 else (3, 2)
                wait_for(first_in.at[chunk, way, d], first_recv.at[chunk, way, d])
                part[chunk, way, dp, half : half + 2] = (
                    to_f32(part[chunk, way, dp, half : half + 2]) + to_f32(first_in[chunk, way, d])
                ).astype(BF16)
                send(
                    part.at[chunk, way, dp, pl.ds(half, 2)],
                    second_in.at[chunk, way, d, pl.ds(half, 2)],
                    main_send, chunk * 16 + 12 + 2 * way + d,
                    second_recv.at[chunk, way, d, 1], along(way, 1 - 2 * d),
                )

    def turn_corner(chunk):
        for way in range(2):
            for d in range(2):
                for late in range(2):
                    half = 2 * ((1 - late + d) % 2)
                    wait_for(
                        second_in.at[chunk, way, d, pl.ds(half, 2)],
                        second_recv.at[chunk, way, d, late],
                    )
            for ds in (2, 1, 3, 0):
                total = (
                    to_f32(part[chunk, way, 0, ds])
                    + to_f32(second_in[chunk, way, 0, ds])
                    + to_f32(second_in[chunk, way, 1, ds])
                ).astype(BF16)
                mid[chunk, way, ds, 0] = total[:, :16]
                mid[chunk, way, ds, 1] = total[:, 16:]
                base = chunk * 12 + way * 6
                axis = 1 - way
                if ds == 2:
                    for d in range(2):
                        send(
                            mid.at[chunk, way, 2, d], third_in.at[chunk, way, d],
                            side_send, base + d, third_recv.at[chunk, way, d],
                            along(axis, 1 - 2 * d),
                        )
                if ds in (1, 3):
                    d, h = (0, 1) if ds == 1 else (1, 0)
                    send(
                        mid.at[chunk, way, ds, h], fourth_in.at[chunk, way, d, h],
                        side_send, base + 2 + d, fourth_recv.at[chunk, way, d, h],
                        along(axis, 1 - 2 * d),
                    )

    def pass_on_side(chunk):
        for way in range(2):
            for d in range(2):
                ds = 1 if d == 0 else 3
                wait_for(third_in.at[chunk, way, d], third_recv.at[chunk, way, d])
                mid[chunk, way, ds, d] = (
                    to_f32(mid[chunk, way, ds, d]) + to_f32(third_in[chunk, way, d])
                ).astype(BF16)
                send(
                    mid.at[chunk, way, ds, d], fourth_in.at[chunk, way, d, d],
                    side_send, chunk * 12 + way * 6 + 4 + d, fourth_recv.at[chunk, way, d, d],
                    along(1 - way, 1 - 2 * d),
                )

    def spread(chunk):
        for way in range(2):
            for d in range(2):
                for h in range(2):
                    wait_for(fourth_in.at[chunk, way, d, h], fourth_recv.at[chunk, way, d, h])
            bases, own_group = [], []
            for h in range(2):
                place = 2 * way + h
                base = pl.multiple_of(target_group(chunk, place) * GROUP, GROUP)
                bases.append(base)
                own_group.append(CHUNKS[chunk][place] == 0)
                row_count = jnp.zeros_like(row)
                for n in range(GROUP):
                    row_count = jnp.where(row >> 1 == n, count_of(base + n), row_count)
                row_valid = 2 * wide + (row & 1) < row_count
                for j in range(J_LOCAL):
                    total = (
                        to_f32(mid[chunk, way, 0, h, j])
                        + to_f32(fourth_in[chunk, way, 0, h, j])
                        + to_f32(fourth_in[chunk, way, 1, h, j])
                    )
                    valid = row_valid & (lane < count_of(rep * J_LOCAL + j))
                    total = jnp.where(valid, total, 0.0).astype(BF16)
                    blocks[pl.ds(base, GROUP), j, :, :] = total.reshape(GROUP, 2, SLOTS)

            def push_to(peer):
                pltpu.make_async_remote_copy(
                    src_ref=blocks.at[peer],
                    dst_ref=blocks_in.at[wide],
                    send_sem=spread_send,
                    recv_sem=spread_recv.at[chunk],
                    device_id={"wide": peer, "rep": rep},
                    device_id_type=MESH,
                ).start()

            def push(step, carry, bases=bases, own_group=own_group):
                for base, near in zip(bases, own_group):
                    push_to(base + (lax.rem(inside + step, GROUP) if near else step))
                return carry

            if own_group[1]:
                push_to(bases[0])
            lax.fori_loop(1 if own_group[1] else 0, GROUP, push, 0)

    def blocks_copy(many, sem):
        return pltpu.make_async_remote_copy(
            src_ref=blocks.at[pl.ds(0, many)],
            dst_ref=blocks_in.at[pl.ds(0, many)],
            send_sem=spread_send,
            recv_sem=sem,
            device_id=along(0, 1),
            device_id_type=MESH,
        )

    amps_load.wait()
    gather_rows(0)
    gather_rows(1)
    ready = 0
    for dx, needed in zip(ORDER, (2, 4, 5, 5)):
        for n in range(ready, needed):
            turn_slab(n)
        ready = needed
        multiply(dx)
        send_parts(0, dx)
        send_parts(1, dx)
        if dx == ORDER[0]:
            pl.semaphore_wait(relay_one, 2)
            tell(relay_two, 2)
    pass_on(0)
    pass_on(1)
    turn_corner(0)
    turn_corner(1)
    pass_on_side(0)
    pass_on_side(1)
    pl.semaphore_wait(relay_two, 2)
    spread(0)
    spread(1)
    own = pltpu.make_async_copy(blocks.at[wide], blocks_in.at[wide], own_sem)
    own.start()
    own.wait()
    for copy in sent:
        copy.wait_send()
    blocks_copy(WIDE - 1, spread_recv.at[0]).wait_send()
    blocks_copy(WIDE // 2, spread_recv.at[0]).wait_recv()
    blocks_copy(WIDE // 2 - 1, spread_recv.at[1]).wait_recv()


def body(amplitudes, integrals, occ_irrep, vir_count):
    dma = pltpu.SemaphoreType.DMA
    out = pl.pallas_call(
        kernel,
        out_shape=jax.ShapeDtypeStruct((WIDE, J_LOCAL, 2, SLOTS), BF16),
        in_specs=[pl.BlockSpec(memory_space=pltpu.HBM)] * 4,
        out_specs=pl.BlockSpec(memory_space=pl.ANY),
        scratch_shapes=[
            pltpu.SMEM((80,), jnp.int32),
            pltpu.SMEM((8,), jnp.int32),
            pltpu.VMEM((WIDE, K_LOCAL, 2, SLOTS), BF16),
            pltpu.VMEM((WIDE, J_LOCAL, 2, SLOTS), BF16),
            pltpu.VMEM((SLABS, K_LOCAL, SLOTS, 16, SLOTS), BF16),
            pltpu.VMEM((80, K_LOCAL * SLOTS, SLOTS), BF16),
            pltpu.VMEM((128, K_LOCAL * SLOTS), BF16),
            pltpu.VMEM((2, 2, 4, 4, J_LOCAL, 32, SLOTS), BF16),
            pltpu.VMEM((2, 2, 2, 2, J_LOCAL, 32, SLOTS), BF16),
            pltpu.VMEM((2, 2, 2, 4, J_LOCAL, 32, SLOTS), BF16),
            pltpu.VMEM((2, 2, 4, 2, J_LOCAL, 16, SLOTS), BF16),
            pltpu.VMEM((2, 2, 2, J_LOCAL, 16, SLOTS), BF16),
            pltpu.VMEM((2, 2, 2, 2, J_LOCAL, 16, SLOTS), BF16),
            dma((K_LOCAL + 3,)),
            dma,
            dma,
            dma((2,)),
            dma((32,)),
            dma((2, 2, 2)),
            dma((2, 2, 2, 2)),
            dma((24,)),
            dma((2, 2, 2)),
            dma((2, 2, 2, 2)),
            pltpu.SemaphoreType.REGULAR,
            pltpu.SemaphoreType.REGULAR,
        ],
        compiler_params=pltpu.CompilerParams(
            collective_id=0, has_side_effects=True, vmem_limit_bytes=63 * 2**20
        ),
        cost_estimate=pl.CostEstimate(
            flops=2 * 128 * 640 * 10240, bytes_accessed=14 * 2**20, transcendentals=0
        ),
    )(amplitudes, integrals, occ_irrep, vir_count)
    return out.transpose(0, 2, 1, 3).reshape(1, 2 * WIDE, J_LOCAL, SLOTS)


def solution(mesh):
    in_specs = (P(None, "rep", "wide", None), P("rep", None, None, None), P(), P())
    out_specs = P("wide", None, "rep", None)
    return jax.shard_map(body, mesh=mesh, in_specs=in_specs, out_specs=out_specs, check_vma=False)
```

```python
import jax
import jax.numpy as jnp
from jax import lax
from jax.experimental import pallas as pl
from jax.experimental.pallas import tpu as pltpu
from jax.sharding import PartitionSpec as P

SYM = 3
MESH = pl.DeviceIdType.MESH
F32 = jnp.float32
BF16 = jnp.bfloat16

WIDE = 64
GROUP = 8
SLOTS = 128
SIDE = 4
K_LOCAL = 5
J_LOCAL = 5
SLABS = 5
ORDER = (2, 3, 1, 0)
CHUNKS = ((3, -3, 4, -2), (2, -1, 1, 0))


def to_f32(value):
    return value.astype(F32)


def kernel(
    amps_hbm, ints_hbm, occ_hbm, vir_hbm, blocks_in,
    occ_ref, vir_ref, amps, blocks, raw, weights, rows, part, first_in, second_in, mid, side_in,
    load_sems, own_sem, spread_send, spread_recv, main_send, first_recv, second_recv,
    side_send, side_recv, relay_one, relay_two,
):
    wide = lax.axis_index("wide")
    rep = lax.axis_index("rep")
    x, y = rep // SIDE, rep % SIDE
    group = wide // GROUP

    amps_load = pltpu.make_async_copy(amps_hbm, amps, load_sems.at[K_LOCAL])
    amps_load.start()
    label_loads = [
        pltpu.make_async_copy(occ_hbm, occ_ref, load_sems.at[K_LOCAL + 1]),
        pltpu.make_async_copy(vir_hbm, vir_ref, load_sems.at[K_LOCAL + 2]),
    ]
    for load in label_loads:
        load.start()
    first_target = lax.rem(x + ORDER[0], SIDE)
    slab = [lax.rem(first_target + n, SLABS) for n in range(SLABS)]
    int_loads = [
        pltpu.make_async_copy(
            ints_hbm.at[:, :, pl.ds(pl.multiple_of(slab[n] * 16, 16), 16), :],
            raw.at[n],
            load_sems.at[n],
        )
        for n in range(SLABS)
    ]
    for load in int_loads:
        load.start()

    def along(axis, step):
        if axis == 0:
            other = lax.rem(x + step + SIDE, SIDE) * SIDE + y
        else:
            other = x * SIDE + lax.rem(y + step + SIDE, SIDE)
        return {"wide": wide, "rep": other}

    barrier = pltpu.get_barrier_semaphore()
    inside = wide - group * GROUP

    def greet(step, carry):
        place = lax.rem(GROUP + inside + step, 3 * GROUP)
        peer = lax.rem(group * GROUP + place - GROUP + WIDE, WIDE)
        pl.semaphore_signal(
            barrier, inc=1, device_id={"wide": peer, "rep": rep}, device_id_type=MESH
        )
        return carry

    def tell(relay, groups):
        for away in (groups, -groups):
            peer = lax.rem(wide + away * GROUP + WIDE, WIDE)
            pl.semaphore_signal(
                relay, inc=1, device_id={"wide": peer, "rep": rep}, device_id_type=MESH
            )

    for axis in range(2):
        for step in (1, 2, 3):
            pl.semaphore_signal(
                barrier, inc=1, device_id=along(axis, step), device_id_type=MESH
            )
    lax.fori_loop(1, 3 * GROUP, greet, 0)
    pl.semaphore_wait(barrier, 3 * GROUP - 1 + 6)
    tell(relay_one, 1)

    def turn_slab(n):
        int_loads[n].wait()
        j = slab[n] * 16

        def turn(step, carry):
            c = pl.multiple_of(step * 16, 16)
            for k in range(K_LOCAL):
                to = pl.multiple_of(k * SLOTS + step * 16, 16)
                weights[pl.ds(j, 16), pl.ds(to, 16), :] = jnp.swapaxes(
                    raw[n, k, pl.ds(c, 16), :, :], 0, 1
                )
            return carry

        lax.fori_loop(0, SLOTS // 16, turn, 0)

    for load in label_loads:
        load.wait()
    lane = lax.broadcasted_iota(jnp.int32, (16, SLOTS), 1)
    row = lax.broadcasted_iota(jnp.int32, (16, SLOTS), 0)

    def count_of(orbital):
        return vir_ref[jnp.bitwise_xor(occ_ref[orbital], SYM)]

    def target_group(chunk, place):
        return lax.rem(group + CHUNKS[chunk][place] + GROUP, GROUP)

    def gather_rows(chunk):
        for k in range(K_LOCAL):
            valid = lane < count_of(rep * K_LOCAL + k)
            for place in range(4):
                at = pl.multiple_of(target_group(chunk, place) * GROUP, GROUP)
                block = amps[pl.ds(at, GROUP), k, :, :].reshape(16, SLOTS)
                at = chunk * 64 + place * 16
                rows[at : at + 16, SLOTS * k : SLOTS * k + SLOTS] = jnp.where(
                    valid, to_f32(block), 0.0
                ).astype(BF16)

    sent = []

    def send(src, dst, sems, index, recv, device):
        copy = pltpu.make_async_remote_copy(
            src_ref=src,
            dst_ref=dst,
            send_sem=sems.at[index],
            recv_sem=recv,
            device_id=device,
            device_id_type=MESH,
        )
        copy.start()
        sent.append(copy)
        return copy

    def multiply(dx):
        def pair(t, carry):
            pieces = []
            ways = (2 + t, 1 - t)
            for dy in ways:
                target = lax.rem(x + dx, SIDE) * SIDE + lax.rem(y + dy, SIDE)
                pieces += [weights[target * J_LOCAL + j] for j in range(J_LOCAL)]
            product = jnp.dot(
                rows[...], jnp.concatenate(pieces, axis=1), preferred_element_type=F32
            ).astype(BF16)
            for n, dy in enumerate(ways):
                for j in range(J_LOCAL):
                    at = (n * J_LOCAL + j) * SLOTS
                    for chunk in range(2):
                        top = chunk * 64
                        part[chunk, 0, dx, dy, j] = product[top : top + 32, at : at + SLOTS]
                        part[chunk, 1, dy, dx, j] = product[top + 32 : top + 64, at : at + SLOTS]
            return carry

        lax.fori_loop(0, 2, pair, 0)

    def send_parts(chunk, dx):
        base = chunk * 16
        if dx == 2:
            for d, half in ((0, 0), (1, 2)):
                send(
                    part.at[chunk, 0, 2, pl.ds(half, 2)], first_in.at[chunk, 0, d],
                    main_send, base + d, first_recv.at[chunk, 0, d], along(0, 1 - 2 * d),
                )
        if dx in (1, 3):
            d, half = (0, 2) if dx == 1 else (1, 0)
            send(
                part.at[chunk, 0, dx, pl.ds(half, 2)],
                second_in.at[chunk, 0, d, pl.ds(half, 2)],
                main_send, base + 2 + d, second_recv.at[chunk, 0, d, 0], along(0, 1 - 2 * d),
            )
        d = 0 if dx < 2 else 1
        send(
            part.at[chunk, 1, 2, dx], first_in.at[chunk, 1, d, dx % 2],
            main_send, base + 4 + dx, first_recv.at[chunk, 1, d], along(1, 1 - 2 * d),
        )
        send(
            part.at[chunk, 1, 1 if d else 3, dx], second_in.at[chunk, 1, 1 - d, dx],
            main_send, base + 8 + dx, second_recv.at[chunk, 1, 1 - d, 0], along(1, 2 * d - 1),
        )

    def wait_for(buffer, sem):
        pltpu.make_async_remote_copy(
            src_ref=buffer, dst_ref=buffer, send_sem=own_sem, recv_sem=sem,
            device_id=along(0, 1), device_id_type=MESH,
        ).wait_recv()

    def pass_on(chunk):
        for way in range(2):
            for d in range(2):
                dp, half = (1, 0) if d == 0 else (3, 2)
                wait_for(first_in.at[chunk, way, d], first_recv.at[chunk, way, d])
                part[chunk, way, dp, half : half + 2] = (
                    to_f32(part[chunk, way, dp, half : half + 2]) + to_f32(first_in[chunk, way, d])
                ).astype(BF16)
                send(
                    part.at[chunk, way, dp, pl.ds(half, 2)],
                    second_in.at[chunk, way, d, pl.ds(half, 2)],
                    main_send, chunk * 16 + 12 + 2 * way + d,
                    second_recv.at[chunk, way, d, 1], along(way, 1 - 2 * d),
                )

    def turn_corner(chunk):
        for way in range(2):
            for d in range(2):
                for late in range(2):
                    half = 2 * ((1 - late + d) % 2)
                    wait_for(
                        second_in.at[chunk, way, d, pl.ds(half, 2)],
                        second_recv.at[chunk, way, d, late],
                    )
            for ds in (2, 1, 3, 0):
                total = (
                    to_f32(part[chunk, way, 0, ds])
                    + to_f32(second_in[chunk, way, 0, ds])
                    + to_f32(second_in[chunk, way, 1, ds])
                ).astype(BF16)
                mid[chunk, way, ds, 0] = total[:, :16]
                mid[chunk, way, ds, 1] = total[:, 16:]
                axis = 1 - way
                if ds:
                    send(
                        mid.at[chunk, way, ds], side_in.at[chunk, way, ds - 1],
                        side_send, chunk * 6 + way * 3 + ds - 1,
                        side_recv.at[chunk, way, ds - 1], along(axis, ds),
                    )

    def spread(chunk):
        for way in range(2):
            for d in range(3):
                wait_for(side_in.at[chunk, way, d], side_recv.at[chunk, way, d])
            bases, own_group = [], []
            for h in range(2):
                place = 2 * way + h
                base = pl.multiple_of(target_group(chunk, place) * GROUP, GROUP)
                bases.append(base)
                own_group.append(CHUNKS[chunk][place] == 0)
                row_count = jnp.zeros_like(row)
                for n in range(GROUP):
                    row_count = jnp.where(row >> 1 == n, count_of(base + n), row_count)
                row_valid = 2 * wide + (row & 1) < row_count
                for j in range(J_LOCAL):
                    total = (
                        to_f32(mid[chunk, way, 0, h, j])
                        + to_f32(side_in[chunk, way, 0, h, j])
                        + to_f32(side_in[chunk, way, 1, h, j])
                        + to_f32(side_in[chunk, way, 2, h, j])
                    )
                    valid = row_valid & (lane < count_of(rep * J_LOCAL + j))
                    total = jnp.where(valid, total, 0.0).astype(BF16)
                    blocks[pl.ds(base, GROUP), j, :, :] = total.reshape(GROUP, 2, SLOTS)

            def push_to(peer):
                pltpu.make_async_remote_copy(
                    src_ref=blocks.at[peer],
                    dst_ref=blocks_in.at[wide],
                    send_sem=spread_send,
                    recv_sem=spread_recv.at[chunk],
                    device_id={"wide": peer, "rep": rep},
                    device_id_type=MESH,
                ).start()

            def push(step, carry, bases=bases, own_group=own_group):
                for base, near in zip(bases, own_group):
                    push_to(base + (lax.rem(inside + step, GROUP) if near else step))
                return carry

            if own_group[1]:
                push_to(bases[0])
            lax.fori_loop(1 if own_group[1] else 0, GROUP, push, 0)

    def blocks_copy(many, sem):
        return pltpu.make_async_remote_copy(
            src_ref=blocks.at[pl.ds(0, many)],
            dst_ref=blocks_in.at[pl.ds(0, many)],
            send_sem=spread_send,
            recv_sem=sem,
            device_id=along(0, 1),
            device_id_type=MESH,
        )

    amps_load.wait()
    gather_rows(0)
    gather_rows(1)
    ready = 0
    for dx, needed in zip(ORDER, (2, 4, 5, 5)):
        for n in range(ready, needed):
            turn_slab(n)
        ready = needed
        multiply(dx)
        send_parts(0, dx)
        send_parts(1, dx)
        if dx == ORDER[0]:
            pl.semaphore_wait(relay_one, 2)
            tell(relay_two, 2)
    pass_on(0)
    pass_on(1)
    turn_corner(0)
    turn_corner(1)
    pl.semaphore_wait(relay_two, 2)
    spread(0)
    spread(1)
    own = pltpu.make_async_copy(blocks.at[wide], blocks_in.at[wide], own_sem)
    own.start()
    own.wait()
    for copy in sent:
        copy.wait_send()
    blocks_copy(WIDE - 1, spread_recv.at[0]).wait_send()
    blocks_copy(WIDE // 2, spread_recv.at[0]).wait_recv()
    blocks_copy(WIDE // 2 - 1, spread_recv.at[1]).wait_recv()


def body(amplitudes, integrals, occ_irrep, vir_count):
    dma = pltpu.SemaphoreType.DMA
    out = pl.pallas_call(
        kernel,
        out_shape=jax.ShapeDtypeStruct((WIDE, J_LOCAL, 2, SLOTS), BF16),
        in_specs=[pl.BlockSpec(memory_space=pltpu.HBM)] * 4,
        out_specs=pl.BlockSpec(memory_space=pl.ANY),
        scratch_shapes=[
            pltpu.SMEM((80,), jnp.int32),
            pltpu.SMEM((8,), jnp.int32),
            pltpu.VMEM((WIDE, K_LOCAL, 2, SLOTS), BF16),
            pltpu.VMEM((WIDE, J_LOCAL, 2, SLOTS), BF16),
            pltpu.VMEM((SLABS, K_LOCAL, SLOTS, 16, SLOTS), BF16),
            pltpu.VMEM((80, K_LOCAL * SLOTS, SLOTS), BF16),
            pltpu.VMEM((128, K_LOCAL * SLOTS), BF16),
            pltpu.VMEM((2, 2, 4, 4, J_LOCAL, 32, SLOTS), BF16),
            pltpu.VMEM((2, 2, 2, 2, J_LOCAL, 32, SLOTS), BF16),
            pltpu.VMEM((2, 2, 2, 4, J_LOCAL, 32, SLOTS), BF16),
            pltpu.VMEM((2, 2, 4, 2, J_LOCAL, 16, SLOTS), BF16),
            pltpu.VMEM((2, 2, 3, 2, J_LOCAL, 16, SLOTS), BF16),
            dma((K_LOCAL + 3,)),
            dma,
            dma,
            dma((2,)),
            dma((32,)),
            dma((2, 2, 2)),
            dma((2, 2, 2, 2)),
            dma((12,)),
            dma((2, 2, 3)),
            pltpu.SemaphoreType.REGULAR,
            pltpu.SemaphoreType.REGULAR,
        ],
        compiler_params=pltpu.CompilerParams(
            collective_id=0, has_side_effects=True, vmem_limit_bytes=63 * 2**20
        ),
        cost_estimate=pl.CostEstimate(
            flops=2 * 128 * 640 * 10240, bytes_accessed=14 * 2**20, transcendentals=0
        ),
    )(amplitudes, integrals, occ_irrep, vir_count)
    return out.transpose(0, 2, 1, 3).reshape(1, 2 * WIDE, J_LOCAL, SLOTS)


def solution(mesh):
    in_specs = (P(None, "rep", "wide", None), P("rep", None, None, None), P(), P())
    out_specs = P("wide", None, "rep", None)
    return jax.shard_map(body, mesh=mesh, in_specs=in_specs, out_specs=out_specs, check_vma=False)
```

```python
import jax
import jax.numpy as jnp
from jax import lax
from jax.experimental import pallas as pl
from jax.experimental.pallas import tpu as pltpu
from jax.sharding import PartitionSpec as P

SYM = 3
MESH = pl.DeviceIdType.MESH
F32 = jnp.float32
BF16 = jnp.bfloat16

WIDE = 64
GROUP = 8
SLOTS = 128
SIDE = 4
K_LOCAL = 5
J_LOCAL = 5
SLABS = 5
ORDER = (2, 3, 1, 0)
CHUNKS = ((3, -3, 4, -2), (2, -1, 1, 0))


def to_f32(value):
    return value.astype(F32)


def kernel(
    amps_hbm, ints_hbm, occ_hbm, vir_hbm, blocks_in,
    occ_ref, vir_ref, amps, blocks, raw, weights, rows, part, first_in, second_in, mid, side_in,
    load_sems, own_sem, spread_send, spread_recv, main_send, first_recv, second_recv,
    side_send, side_recv, relay_one, relay_two,
):
    wide = lax.axis_index("wide")
    rep = lax.axis_index("rep")
    x, y = rep // SIDE, rep % SIDE
    group = wide // GROUP

    amps_load = pltpu.make_async_copy(amps_hbm, amps, load_sems.at[K_LOCAL])
    amps_load.start()
    label_loads = [
        pltpu.make_async_copy(occ_hbm, occ_ref, load_sems.at[K_LOCAL + 1]),
        pltpu.make_async_copy(vir_hbm, vir_ref, load_sems.at[K_LOCAL + 2]),
    ]
    for load in label_loads:
        load.start()
    first_target = lax.rem(x + ORDER[0], SIDE)
    slab = [lax.rem(first_target + n, SLABS) for n in range(SLABS)]
    int_loads = [
        pltpu.make_async_copy(
            ints_hbm.at[:, :, pl.ds(pl.multiple_of(slab[n] * 16, 16), 16), :],
            raw.at[n],
            load_sems.at[n],
        )
        for n in range(SLABS)
    ]
    for load in int_loads:
        load.start()

    def along(axis, step):
        if axis == 0:
            other = lax.rem(x + step + SIDE, SIDE) * SIDE + y
        else:
            other = x * SIDE + lax.rem(y + step + SIDE, SIDE)
        return {"wide": wide, "rep": other}

    barrier = pltpu.get_barrier_semaphore()
    inside = wide - group * GROUP

    def greet(step, carry):
        place = lax.rem(GROUP + inside + step, 3 * GROUP)
        peer = lax.rem(group * GROUP + place - GROUP + WIDE, WIDE)
        pl.semaphore_signal(
            barrier, inc=1, device_id={"wide": peer, "rep": rep}, device_id_type=MESH
        )
        return carry

    def tell(relay, groups):
        for away in (groups, -groups):
            peer = lax.rem(wide + away * GROUP + WIDE, WIDE)
            pl.semaphore_signal(
                relay, inc=1, device_id={"wide": peer, "rep": rep}, device_id_type=MESH
            )

    for axis in range(2):
        for step in (1, 2, 3):
            pl.semaphore_signal(
                barrier, inc=1, device_id=along(axis, step), device_id_type=MESH
            )
    lax.fori_loop(1, 3 * GROUP, greet, 0)
    pl.semaphore_wait(barrier, 3 * GROUP - 1 + 6)
    tell(relay_one, 1)

    def turn_slab(n):
        int_loads[n].wait()
        j = slab[n] * 16

        def turn(step, carry):
            c = pl.multiple_of(step * 16, 16)
            for k in range(K_LOCAL):
                to = pl.multiple_of(k * SLOTS + step * 16, 16)
                weights[pl.ds(j, 16), pl.ds(to, 16), :] = jnp.swapaxes(
                    raw[n, k, pl.ds(c, 16), :, :], 0, 1
                )
            return carry

        lax.fori_loop(0, SLOTS // 16, turn, 0)

    for load in label_loads:
        load.wait()
    lane = lax.broadcasted_iota(jnp.int32, (16, SLOTS), 1)
    row = lax.broadcasted_iota(jnp.int32, (16, SLOTS), 0)

    def count_of(orbital):
        return vir_ref[jnp.bitwise_xor(occ_ref[orbital], SYM)]

    def target_group(chunk, place):
        return lax.rem(group + CHUNKS[chunk][place] + GROUP, GROUP)

    def gather_rows(chunk):
        for k in range(K_LOCAL):
            valid = lane < count_of(rep * K_LOCAL + k)
            for place in range(4):
                at = pl.multiple_of(target_group(chunk, place) * GROUP, GROUP)
                block = amps[pl.ds(at, GROUP), k, :, :].reshape(16, SLOTS)
                at = chunk * 64 + place * 16
                rows[at : at + 16, SLOTS * k : SLOTS * k + SLOTS] = jnp.where(
                    valid, to_f32(block), 0.0
                ).astype(BF16)

    sent = []

    def send(src, dst, sems, index, recv, device):
        copy = pltpu.make_async_remote_copy(
            src_ref=src,
            dst_ref=dst,
            send_sem=sems.at[index],
            recv_sem=recv,
            device_id=device,
            device_id_type=MESH,
        )
        copy.start()
        sent.append(copy)
        return copy

    def multiply(dx):
        def pair(t, carry):
            pieces = []
            ways = (2 + t, 1 - t)
            for dy in ways:
                target = lax.rem(x + dx, SIDE) * SIDE + lax.rem(y + dy, SIDE)
                pieces += [weights[target * J_LOCAL + j] for j in range(J_LOCAL)]
            product = jnp.dot(
                rows[...], jnp.concatenate(pieces, axis=1), preferred_element_type=F32
            ).astype(BF16)
            for n, dy in enumerate(ways):
                for j in range(J_LOCAL):
                    at = (n * J_LOCAL + j) * SLOTS
                    for chunk in range(2):
                        top = chunk * 64
                        part[chunk, 0, dx, dy, j] = product[top : top + 32, at : at + SLOTS]
                        part[chunk, 1, dy, dx, j] = product[top + 32 : top + 64, at : at + SLOTS]
            return carry

        lax.fori_loop(0, 2, pair, 0)

    def send_parts(chunk, dx):
        base = chunk * 16
        if dx == 2:
            for d, half in ((0, 0), (1, 2)):
                send(
                    part.at[chunk, 0, 2, pl.ds(half, 2)], first_in.at[chunk, 0, d],
                    main_send, base + d, first_recv.at[chunk, 0, d], along(0, 1 - 2 * d),
                )
        if dx in (1, 3):
            d, half = (0, 2) if dx == 1 else (1, 0)
            send(
                part.at[chunk, 0, dx, pl.ds(half, 2)],
                second_in.at[chunk, 0, d, pl.ds(half, 2)],
                main_send, base + 2 + d, second_recv.at[chunk, 0, d, 0], along(0, 1 - 2 * d),
            )
        d = 0 if dx < 2 else 1
        send(
            part.at[chunk, 1, 2, dx], first_in.at[chunk, 1, d, dx % 2],
            main_send, base + 4 + dx, first_recv.at[chunk, 1, d], along(1, 1 - 2 * d),
        )
        send(
            part.at[chunk, 1, 1 if d else 3, dx], second_in.at[chunk, 1, 1 - d, dx],
            main_send, base + 8 + dx, second_recv.at[chunk, 1, 1 - d, 0], along(1, 2 * d - 1),
        )

    def wait_for(buffer, sem):
        pltpu.make_async_remote_copy(
            src_ref=buffer, dst_ref=buffer, send_sem=own_sem, recv_sem=sem,
            device_id=along(0, 1), device_id_type=MESH,
        ).wait_recv()

    def pass_on(chunk):
        for way in range(2):
            for d in range(2):
                dp, half = (1, 0) if d == 0 else (3, 2)
                wait_for(first_in.at[chunk, way, d], first_recv.at[chunk, way, d])
                part[chunk, way, dp, half : half + 2] = (
                    to_f32(part[chunk, way, dp, half : half + 2]) + to_f32(first_in[chunk, way, d])
                ).astype(BF16)
                send(
                    part.at[chunk, way, dp, pl.ds(half, 2)],
                    second_in.at[chunk, way, d, pl.ds(half, 2)],
                    main_send, chunk * 16 + 12 + 2 * way + d,
                    second_recv.at[chunk, way, d, 1], along(way, 1 - 2 * d),
                )

    def turn_corner(chunk):
        for way in range(2):
            for d in range(2):
                for late in range(2):
                    half = 2 * ((1 - late + d) % 2)
                    wait_for(
                        second_in.at[chunk, way, d, pl.ds(half, 2)],
                        second_recv.at[chunk, way, d, late],
                    )
            for ds in (2, 1, 3, 0):
                total = (
                    to_f32(part[chunk, way, 0, ds])
                    + to_f32(second_in[chunk, way, 0, ds])
                    + to_f32(second_in[chunk, way, 1, ds])
                ).astype(BF16)
                mid[chunk, way, ds, 0] = total[:, :16]
                mid[chunk, way, ds, 1] = total[:, 16:]
                axis = 1 - way
                if ds:
                    send(
                        mid.at[chunk, way, ds], side_in.at[chunk, way, ds - 1],
                        side_send, chunk * 6 + way * 3 + ds - 1,
                        side_recv.at[chunk, way, ds - 1], along(axis, ds),
                    )

    def spread(chunk):
        for way in range(2):
            for d in range(3):
                wait_for(side_in.at[chunk, way, d], side_recv.at[chunk, way, d])
            bases, own_group = [], []
            for h in range(2):
                place = 2 * way + h
                base = pl.multiple_of(target_group(chunk, place) * GROUP, GROUP)
                bases.append(base)
                own_group.append(CHUNKS[chunk][place] == 0)
                row_count = jnp.zeros_like(row)
                for n in range(GROUP):
                    row_count = jnp.where(row >> 1 == n, count_of(base + n), row_count)
                row_valid = 2 * wide + (row & 1) < row_count
                for j in range(J_LOCAL):
                    total = (
                        to_f32(mid[chunk, way, 0, h, j])
                        + to_f32(side_in[chunk, way, 0, h, j])
                        + to_f32(side_in[chunk, way, 1, h, j])
                        + to_f32(side_in[chunk, way, 2, h, j])
                    )
                    valid = row_valid & (lane < count_of(rep * J_LOCAL + j))
                    total = jnp.where(valid, total, 0.0).astype(BF16)
                    blocks[pl.ds(base, GROUP), j, :, :] = total.reshape(GROUP, 2, SLOTS)

            def push_to(peer):
                pltpu.make_async_remote_copy(
                    src_ref=blocks.at[peer],
                    dst_ref=blocks_in.at[wide],
                    send_sem=spread_send,
                    recv_sem=spread_recv.at[chunk],
                    device_id={"wide": peer, "rep": rep},
                    device_id_type=MESH,
                ).start()

            def push(step, carry, bases=bases, own_group=own_group):
                for base, near in zip(bases, own_group):
                    push_to(base + (lax.rem(inside + step, GROUP) if near else step))
                return carry

            if own_group[1]:
                push_to(bases[0])
            lax.fori_loop(1 if own_group[1] else 0, GROUP, push, 0)

    def blocks_copy(many, sem):
        return pltpu.make_async_remote_copy(
            src_ref=blocks.at[pl.ds(0, many)],
            dst_ref=blocks_in.at[pl.ds(0, many)],
            send_sem=spread_send,
            recv_sem=sem,
            device_id=along(0, 1),
            device_id_type=MESH,
        )

    amps_load.wait()
    gather_rows(0)
    gather_rows(1)
    ready = 0
    for dx, needed in zip(ORDER, (2, 4, 5, 5)):
        for n in range(ready, needed):
            turn_slab(n)
        ready = needed
        multiply(dx)
        send_parts(0, dx)
        if dx == ORDER[0]:
            pl.semaphore_wait(relay_one, 2)
            tell(relay_two, 2)
    pass_on(0)
    for dx in ORDER:
        send_parts(1, dx)
    turn_corner(0)
    pass_on(1)
    pl.semaphore_wait(relay_two, 2)
    spread(0)
    turn_corner(1)
    spread(1)
    own = pltpu.make_async_copy(blocks.at[wide], blocks_in.at[wide], own_sem)
    own.start()
    own.wait()
    for copy in sent:
        copy.wait_send()
    blocks_copy(WIDE - 1, spread_recv.at[0]).wait_send()
    blocks_copy(WIDE // 2, spread_recv.at[0]).wait_recv()
    blocks_copy(WIDE // 2 - 1, spread_recv.at[1]).wait_recv()


def body(amplitudes, integrals, occ_irrep, vir_count):
    dma = pltpu.SemaphoreType.DMA
    out = pl.pallas_call(
        kernel,
        out_shape=jax.ShapeDtypeStruct((WIDE, J_LOCAL, 2, SLOTS), BF16),
        in_specs=[pl.BlockSpec(memory_space=pltpu.HBM)] * 4,
        out_specs=pl.BlockSpec(memory_space=pl.ANY),
        scratch_shapes=[
            pltpu.SMEM((80,), jnp.int32),
            pltpu.SMEM((8,), jnp.int32),
            pltpu.VMEM((WIDE, K_LOCAL, 2, SLOTS), BF16),
            pltpu.VMEM((WIDE, J_LOCAL, 2, SLOTS), BF16),
            pltpu.VMEM((SLABS, K_LOCAL, SLOTS, 16, SLOTS), BF16),
            pltpu.VMEM((80, K_LOCAL * SLOTS, SLOTS), BF16),
            pltpu.VMEM((128, K_LOCAL * SLOTS), BF16),
            pltpu.VMEM((2, 2, 4, 4, J_LOCAL, 32, SLOTS), BF16),
            pltpu.VMEM((2, 2, 2, 2, J_LOCAL, 32, SLOTS), BF16),
            pltpu.VMEM((2, 2, 2, 4, J_LOCAL, 32, SLOTS), BF16),
            pltpu.VMEM((2, 2, 4, 2, J_LOCAL, 16, SLOTS), BF16),
            pltpu.VMEM((2, 2, 3, 2, J_LOCAL, 16, SLOTS), BF16),
            dma((K_LOCAL + 3,)),
            dma,
            dma,
            dma((2,)),
            dma((32,)),
            dma((2, 2, 2)),
            dma((2, 2, 2, 2)),
            dma((12,)),
            dma((2, 2, 3)),
            pltpu.SemaphoreType.REGULAR,
            pltpu.SemaphoreType.REGULAR,
        ],
        compiler_params=pltpu.CompilerParams(
            collective_id=0, has_side_effects=True, vmem_limit_bytes=63 * 2**20
        ),
        cost_estimate=pl.CostEstimate(
            flops=2 * 128 * 640 * 10240, bytes_accessed=14 * 2**20, transcendentals=0
        ),
    )(amplitudes, integrals, occ_irrep, vir_count)
    return out.transpose(0, 2, 1, 3).reshape(1, 2 * WIDE, J_LOCAL, SLOTS)


def solution(mesh):
    in_specs = (P(None, "rep", "wide", None), P("rep", None, None, None), P(), P())
    out_specs = P("wide", None, "rep", None)
    return jax.shard_map(body, mesh=mesh, in_specs=in_specs, out_specs=out_specs, check_vma=False)
```

```python
import jax
import jax.numpy as jnp
from jax import lax
from jax.experimental import pallas as pl
from jax.experimental.pallas import tpu as pltpu
from jax.sharding import PartitionSpec as P

SYM = 3
MESH = pl.DeviceIdType.MESH
F32 = jnp.float32
BF16 = jnp.bfloat16

WIDE = 64
GROUP = 8
SLOTS = 128
SIDE = 4
K_LOCAL = 5
J_LOCAL = 5
SLABS = 5
ORDER = (2, 3, 1, 0)
CHUNKS = ((4, -2, 3, -3), (2, -1, 1, 0))


def to_f32(value):
    return value.astype(F32)


def kernel(
    amps_hbm, ints_hbm, occ_hbm, vir_hbm, blocks_in,
    occ_ref, vir_ref, amps, blocks, raw, weights, rows, part, first_in, second_in, mid, side_in,
    load_sems, own_sem, spread_send, spread_recv, main_send, first_recv, second_recv,
    side_send, side_recv, relay_one, relay_two,
):
    wide = lax.axis_index("wide")
    rep = lax.axis_index("rep")
    x, y = rep // SIDE, rep % SIDE
    group = wide // GROUP

    amps_load = pltpu.make_async_copy(amps_hbm, amps, load_sems.at[K_LOCAL])
    amps_load.start()
    label_loads = [
        pltpu.make_async_copy(occ_hbm, occ_ref, load_sems.at[K_LOCAL + 1]),
        pltpu.make_async_copy(vir_hbm, vir_ref, load_sems.at[K_LOCAL + 2]),
    ]
    for load in label_loads:
        load.start()
    first_target = lax.rem(x + ORDER[0], SIDE)
    slab = [lax.rem(first_target + n, SLABS) for n in range(SLABS)]
    int_loads = [
        pltpu.make_async_copy(
            ints_hbm.at[:, :, pl.ds(pl.multiple_of(slab[n] * 16, 16), 16), :],
            raw.at[n],
            load_sems.at[n],
        )
        for n in range(SLABS)
    ]
    for load in int_loads:
        load.start()

    def along(axis, step):
        if axis == 0:
            other = lax.rem(x + step + SIDE, SIDE) * SIDE + y
        else:
            other = x * SIDE + lax.rem(y + step + SIDE, SIDE)
        return {"wide": wide, "rep": other}

    barrier = pltpu.get_barrier_semaphore()
    inside = wide - group * GROUP

    def greet(step, carry):
        place = lax.rem(GROUP + inside + step, 3 * GROUP)
        peer = lax.rem(group * GROUP + place - GROUP + WIDE, WIDE)
        pl.semaphore_signal(
            barrier, inc=1, device_id={"wide": peer, "rep": rep}, device_id_type=MESH
        )
        return carry

    def tell(relay, groups):
        for away in (groups, -groups):
            peer = lax.rem(wide + away * GROUP + WIDE, WIDE)
            pl.semaphore_signal(
                relay, inc=1, device_id={"wide": peer, "rep": rep}, device_id_type=MESH
            )

    for axis in range(2):
        for step in (1, 2, 3):
            pl.semaphore_signal(
                barrier, inc=1, device_id=along(axis, step), device_id_type=MESH
            )
    lax.fori_loop(1, 3 * GROUP, greet, 0)
    pl.semaphore_wait(barrier, 3 * GROUP - 1 + 6)
    tell(relay_one, 1)

    def turn_slab(n):
        int_loads[n].wait()
        j = slab[n] * 16

        def turn(step, carry):
            c = pl.multiple_of(step * 16, 16)
            for k in range(K_LOCAL):
                to = pl.multiple_of(k * SLOTS + step * 16, 16)
                weights[pl.ds(j, 16), pl.ds(to, 16), :] = jnp.swapaxes(
                    raw[n, k, pl.ds(c, 16), :, :], 0, 1
                )
            return carry

        lax.fori_loop(0, SLOTS // 16, turn, 0)

    for load in label_loads:
        load.wait()
    lane = lax.broadcasted_iota(jnp.int32, (16, SLOTS), 1)
    row = lax.broadcasted_iota(jnp.int32, (16, SLOTS), 0)

    def count_of(orbital):
        return vir_ref[jnp.bitwise_xor(occ_ref[orbital], SYM)]

    def target_group(chunk, place):
        return lax.rem(group + CHUNKS[chunk][place] + GROUP, GROUP)

    def gather_rows(chunk):
        for k in range(K_LOCAL):
            valid = lane < count_of(rep * K_LOCAL + k)
            for place in range(4):
                at = pl.multiple_of(target_group(chunk, place) * GROUP, GROUP)
                block = amps[pl.ds(at, GROUP), k, :, :].reshape(16, SLOTS)
                at = chunk * 64 + place * 16
                rows[at : at + 16, SLOTS * k : SLOTS * k + SLOTS] = jnp.where(
                    valid, to_f32(block), 0.0
                ).astype(BF16)

    sent = []

    def send(src, dst, sems, index, recv, device):
        copy = pltpu.make_async_remote_copy(
            src_ref=src,
            dst_ref=dst,
            send_sem=sems.at[index],
            recv_sem=recv,
            device_id=device,
            device_id_type=MESH,
        )
        copy.start()
        sent.append(copy)
        return copy

    def multiply(dx):
        def pair(t, carry):
            pieces = []
            ways = (2 + t, 1 - t)
            for dy in ways:
                target = lax.rem(x + dx, SIDE) * SIDE + lax.rem(y + dy, SIDE)
                pieces += [weights[target * J_LOCAL + j] for j in range(J_LOCAL)]
            product = jnp.dot(
                rows[...], jnp.concatenate(pieces, axis=1), preferred_element_type=F32
            ).astype(BF16)
            for n, dy in enumerate(ways):
                for j in range(J_LOCAL):
                    at = (n * J_LOCAL + j) * SLOTS
                    for chunk in range(2):
                        top = chunk * 64
                        part[chunk, 0, dx, dy, j] = product[top : top + 32, at : at + SLOTS]
                        part[chunk, 1, dy, dx, j] = product[top + 32 : top + 64, at : at + SLOTS]
            return carry

        lax.fori_loop(0, 2, pair, 0)

    def send_parts(chunk, dx):
        base = chunk * 16
        if dx == 2:
            for d, half in ((0, 0), (1, 2)):
                send(
                    part.at[chunk, 0, 2, pl.ds(half, 2)], first_in.at[chunk, 0, d],
                    main_send, base + d, first_recv.at[chunk, 0, d], along(0, 1 - 2 * d),
                )
        if dx in (1, 3):
            d, half = (0, 2) if dx == 1 else (1, 0)
            send(
                part.at[chunk, 0, dx, pl.ds(half, 2)],
                second_in.at[chunk, 0, d, pl.ds(half, 2)],
                main_send, base + 2 + d, second_recv.at[chunk, 0, d, 0], along(0, 1 - 2 * d),
            )
        d = 0 if dx < 2 else 1
        send(
            part.at[chunk, 1, 2, dx], first_in.at[chunk, 1, d, dx % 2],
            main_send, base + 4 + dx, first_recv.at[chunk, 1, d], along(1, 1 - 2 * d),
        )
        send(
            part.at[chunk, 1, 1 if d else 3, dx], second_in.at[chunk, 1, 1 - d, dx],
            main_send, base + 8 + dx, second_recv.at[chunk, 1, 1 - d, 0], along(1, 2 * d - 1),
        )

    def wait_for(buffer, sem):
        pltpu.make_async_remote_copy(
            src_ref=buffer, dst_ref=buffer, send_sem=own_sem, recv_sem=sem,
            device_id=along(0, 1), device_id_type=MESH,
        ).wait_recv()

    def pass_on(chunk):
        for way in range(2):
            for d in range(2):
                dp, half = (1, 0) if d == 0 else (3, 2)
                wait_for(first_in.at[chunk, way, d], first_recv.at[chunk, way, d])
                part[chunk, way, dp, half : half + 2] = (
                    part[chunk, way, dp, half : half + 2] + first_in[chunk, way, d]
                )
                send(
                    part.at[chunk, way, dp, pl.ds(half, 2)],
                    second_in.at[chunk, way, d, pl.ds(half, 2)],
                    main_send, chunk * 16 + 12 + 2 * way + d,
                    second_recv.at[chunk, way, d, 1], along(way, 1 - 2 * d),
                )

    def turn_corner(chunk):
        for way in range(2):
            for d in range(2):
                for late in range(2):
                    half = 2 * ((1 - late + d) % 2)
                    wait_for(
                        second_in.at[chunk, way, d, pl.ds(half, 2)],
                        second_recv.at[chunk, way, d, late],
                    )
            for ds in (2, 1, 3, 0):
                total = (
                    to_f32(part[chunk, way, 0, ds])
                    + to_f32(second_in[chunk, way, 0, ds])
                    + to_f32(second_in[chunk, way, 1, ds])
                ).astype(BF16)
                mid[chunk, way, ds, 0] = total[:, :16]
                mid[chunk, way, ds, 1] = total[:, 16:]
                axis = 1 - way
                if ds:
                    send(
                        mid.at[chunk, way, ds], side_in.at[chunk, way, ds - 1],
                        side_send, chunk * 6 + way * 3 + ds - 1,
                        side_recv.at[chunk, way, ds - 1], along(axis, ds),
                    )

    def spread(chunk):
        for way in range(2):
            for d in range(3):
                wait_for(side_in.at[chunk, way, d], side_recv.at[chunk, way, d])
            bases, own_group = [], []
            for h in range(2):
                place = 2 * way + h
                base = pl.multiple_of(target_group(chunk, place) * GROUP, GROUP)
                bases.append(base)
                own_group.append(CHUNKS[chunk][place] == 0)
                row_count = jnp.zeros_like(row)
                for n in range(GROUP):
                    row_count = jnp.where(row >> 1 == n, count_of(base + n), row_count)
                row_valid = 2 * wide + (row & 1) < row_count
                for j in range(J_LOCAL):
                    total = (
                        to_f32(mid[chunk, way, 0, h, j])
                        + to_f32(side_in[chunk, way, 0, h, j])
                        + to_f32(side_in[chunk, way, 1, h, j])
                        + to_f32(side_in[chunk, way, 2, h, j])
                    )
                    valid = row_valid & (lane < count_of(rep * J_LOCAL + j))
                    total = jnp.where(valid, total, 0.0).astype(BF16)
                    blocks[pl.ds(base, GROUP), j, :, :] = total.reshape(GROUP, 2, SLOTS)

            def push_to(peer):
                pltpu.make_async_remote_copy(
                    src_ref=blocks.at[peer],
                    dst_ref=blocks_in.at[wide],
                    send_sem=spread_send,
                    recv_sem=spread_recv.at[chunk],
                    device_id={"wide": peer, "rep": rep},
                    device_id_type=MESH,
                ).start()

            def push(step, carry, bases=bases, own_group=own_group):
                for base, near in zip(bases, own_group):
                    push_to(base + (lax.rem(inside + step, GROUP) if near else step))
                return carry

            if own_group[1]:
                push_to(bases[0])
            lax.fori_loop(1 if own_group[1] else 0, GROUP, push, 0)

    def blocks_copy(many, sem):
        return pltpu.make_async_remote_copy(
            src_ref=blocks.at[pl.ds(0, many)],
            dst_ref=blocks_in.at[pl.ds(0, many)],
            send_sem=spread_send,
            recv_sem=sem,
            device_id=along(0, 1),
            device_id_type=MESH,
        )

    amps_load.wait()
    gather_rows(0)
    gather_rows(1)
    ready = 0
    for dx, needed in zip(ORDER, (2, 4, 5, 5)):
        for n in range(ready, needed):
            turn_slab(n)
        ready = needed
        multiply(dx)
        send_parts(0, dx)
        send_parts(1, dx)
        if dx == ORDER[0]:
            pl.semaphore_wait(relay_one, 2)
            tell(relay_two, 2)
    pass_on(0)
    pass_on(1)
    turn_corner(0)
    turn_corner(1)
    pl.semaphore_wait(relay_two, 2)
    spread(0)
    spread(1)
    own = pltpu.make_async_copy(blocks.at[wide], blocks_in.at[wide], own_sem)
    own.start()
    own.wait()
    for copy in sent:
        copy.wait_send()
    blocks_copy(WIDE - 1, spread_recv.at[0]).wait_send()
    blocks_copy(WIDE // 2, spread_recv.at[0]).wait_recv()
    blocks_copy(WIDE // 2 - 1, spread_recv.at[1]).wait_recv()


def body(amplitudes, integrals, occ_irrep, vir_count):
    dma = pltpu.SemaphoreType.DMA
    out = pl.pallas_call(
        kernel,
        out_shape=jax.ShapeDtypeStruct((WIDE, J_LOCAL, 2, SLOTS), BF16),
        in_specs=[pl.BlockSpec(memory_space=pltpu.HBM)] * 4,
        out_specs=pl.BlockSpec(memory_space=pl.ANY),
        scratch_shapes=[
            pltpu.SMEM((80,), jnp.int32),
            pltpu.SMEM((8,), jnp.int32),
            pltpu.VMEM((WIDE, K_LOCAL, 2, SLOTS), BF16),
            pltpu.VMEM((WIDE, J_LOCAL, 2, SLOTS), BF16),
            pltpu.VMEM((SLABS, K_LOCAL, SLOTS, 16, SLOTS), BF16),
            pltpu.VMEM((80, K_LOCAL * SLOTS, SLOTS), BF16),
            pltpu.VMEM((128, K_LOCAL * SLOTS), BF16),
            pltpu.VMEM((2, 2, 4, 4, J_LOCAL, 32, SLOTS), BF16),
            pltpu.VMEM((2, 2, 2, 2, J_LOCAL, 32, SLOTS), BF16),
            pltpu.VMEM((2, 2, 2, 4, J_LOCAL, 32, SLOTS), BF16),
            pltpu.VMEM((2, 2, 4, 2, J_LOCAL, 16, SLOTS), BF16),
            pltpu.VMEM((2, 2, 3, 2, J_LOCAL, 16, SLOTS), BF16),
            dma((K_LOCAL + 3,)),
            dma,
            dma,
            dma((2,)),
            dma((32,)),
            dma((2, 2, 2)),
            dma((2, 2, 2, 2)),
            dma((12,)),
            dma((2, 2, 3)),
            pltpu.SemaphoreType.REGULAR,
            pltpu.SemaphoreType.REGULAR,
        ],
        compiler_params=pltpu.CompilerParams(
            collective_id=0, has_side_effects=True, vmem_limit_bytes=63 * 2**20
        ),
        cost_estimate=pl.CostEstimate(
            flops=2 * 128 * 640 * 10240, bytes_accessed=14 * 2**20, transcendentals=0
        ),
    )(amplitudes, integrals, occ_irrep, vir_count)
    return out.transpose(0, 2, 1, 3).reshape(1, 2 * WIDE, J_LOCAL, SLOTS)


def solution(mesh):
    in_specs = (P(None, "rep", "wide", None), P("rep", None, None, None), P(), P())
    out_specs = P("wide", None, "rep", None)
    return jax.shard_map(body, mesh=mesh, in_specs=in_specs, out_specs=out_specs, check_vma=False)
```
